512 devices in a mesh: ctx: 16 (over z), ch: 32 (over y, x, core).
Axes of the slice: x: 4, y: 4, z: 16, core: 2. Of those that a mesh axis runs over, the one named last changes fastest.
Arguments:
- resid_in: bfloat16 [2048, 4096], P('ctx', 'ch'), may hold values from -800 to 800
- query_in: bfloat16 [2048, 4096], P('ctx', 'ch'), may hold values from -6 to 6
- key_in: bfloat16 [2048, 4096], P('ctx', 'ch'), may hold values from -6 to 6
- value_in: bfloat16 [2048, 4096], P('ctx', 'ch'), may hold values from -6 to 6
- filt: float32 [4096, 2048], P(('ch', 'ctx')), may hold values from -4 to 4
- gain: float32 [4096], P('ch'), may hold values from 0.5 to 1.5
- w_gate: bfloat16 [4096, 11008], P('ctx', 'ch'), may hold values from -0.09375 to 0.09375
- w_up: bfloat16 [4096, 11008], P('ctx', 'ch'), may hold values from -0.09375 to 0.09375
- g_hid: bfloat16 [2048, 11008], P('ctx', 'ch'), may hold values from -6 to 6
- g_res: bfloat16 [2048, 4096], P('ctx', 'ch'), may hold values from -1.5 to 1.5
Outputs:
- dx: bfloat16 [2048, 4096], P('ctx', 'ch')
- dq: bfloat16 [2048, 4096], P('ctx', 'ch')
- dk: bfloat16 [2048, 4096], P('ctx', 'ch')
- dv: bfloat16 [2048, 4096], P('ctx', 'ch')
- dfilt: float32 [4096, 2048], P(('ch', 'ctx'))
- dgain: float32 [4096], P('ch')
- dw_gate: float32 [4096, 11008], P('ctx', 'ch')
- dw_up: float32 [4096, 11008], P('ctx', 'ch')
- amax: float32 [], replicated
The draws below stay inside these ranges and needn't reach their ends.
All inputs are finite; a program needn't handle non-finite values.
Results may differ from the reference program's by a relative error of at most 0.025.
Values may be sent and summed in bfloat16 or wider, within the bound.
No kernel may reach another device: no remote copies, remote signals or barrier semaphores. Data moves between devices by JAX's collectives and lax.ppermute only.
A program may use at most 64 MiB of HBM per device.

```python
import jax
import jax.numpy as jnp
from jax import lax

D = 4096
FF = 11008
L = 2048
N_CH = 32


def draw_resid_in(key, part):
    key = jax.random.fold_in(key, 5)
    key_base, key_where, key_size, key_sign, key_top = jax.random.split(key, 5)
    base = jnp.clip(jax.random.normal(key_base, (L, D), jnp.float32), -4.0, 4.0)
    rise = 3.0
    level = 2.15
    chan_scale = rise ** (jnp.arange(D, dtype=jnp.float32) / D)
    where = jax.random.randint(key_where, (L,), 0, D)
    top = jax.random.randint(key_top, (), 0, L)
    rows = jnp.arange(L, dtype=jnp.int32)
    ratio = jax.random.uniform(key_size, (L,), jnp.float32, 0.4, 0.6)
    ratio = jnp.where(rows == top, ratio + 2.3, ratio)
    sign = jnp.where(jax.random.randint(key_sign, (L,), 0, 2) == 1, 1.0, -1.0)
    height = level * jnp.sqrt(D * 1.0) * ratio * sign
    onehot = (where[:, None] == jnp.arange(D, dtype=jnp.int32)[None, :]).astype(jnp.float32)
    return (base * chan_scale[None, :] + onehot * height[:, None]).astype(jnp.bfloat16)


def draw_filt(key, part):
    key = jax.random.fold_in(key, 11)
    key_rate, key_rough = jax.random.split(key)
    low = jnp.log(30.0)
    rough = jnp.clip(jax.random.normal(key_rough, (D, L), jnp.float32), -4.0, 4.0)
    high = jnp.log(8.0 * L)
    tau = jnp.exp(jax.random.uniform(key_rate, (D, 1), jnp.float32, low, high))
    steps = jnp.arange(L, dtype=jnp.float32)[None, :]
    norm = jnp.sqrt((1.0 - jnp.exp(-2.0 * L / tau)) / (1.0 - jnp.exp(-2.0 / tau)))
    return rough * jnp.exp(-steps / tau) / norm


def level_of(stream_key, shape, shards, least, high):
    level = 1.0
    for dim, parts in shards:
        heights = jax.random.uniform(jax.random.fold_in(jax.random.fold_in(stream_key, 6), dim), (parts,), jnp.float32, least / len(shards), high / len(shards))
        level = level * jnp.repeat(jnp.exp(heights), shape[dim] // parts).reshape((-1,) + (1,) * (len(shape) - 1 - dim))
    return level


def noise(stream_key, extent, scale, reach, pieces=(), held_as=jnp.bfloat16):
    loudness = level_of(stream_key, extent, pieces, -0.22, 0.18) if pieces else 1.0
    values = jax.random.normal(stream_key, extent, jnp.float32) * scale * loudness
    return jnp.minimum(jnp.maximum(values, -reach), reach).astype(held_as)


def setup_inputs(seed: int = 0) -> dict:
    seeds = jax.random.split(jax.random.key(seed), 11)
    resid_in = draw_resid_in(jax.random.fold_in(seeds[10], 71), 0)
    query_in = noise(seeds[1], (L, D), 1.0, 6.0, ((0, 16), (1, 32)))
    key_in = noise(seeds[2], (L, D), 1.0, 6.0, ((0, 16), (1, 32)))
    value_in = noise(seeds[3], (L, D), 1.0, 6.0, ((0, 16), (1, 32)))
    filt = draw_filt(jax.random.fold_in(seeds[10], 71), 0)
    gain = jnp.clip(1.0 + 0.1 * jax.random.normal(seeds[5], (D,), jnp.float32), 0.5, 1.5)
    w_gate = noise(seeds[6], (D, FF), D ** -0.5, 0.09375, ((0, 16), (1, 32)))
    w_up = noise(seeds[7], (D, FF), D ** -0.5, 0.09375, ((0, 16), (1, 32)))
    g_hid = noise(seeds[8], (L, FF), 1.0, 6.0, ((0, 16), (1, 32)))
    g_res = noise(seeds[9], (L, D), 0.1, 1.5, ((0, 16), (1, 32)))
    return {"resid_in": resid_in, "query_in": query_in, "key_in": key_in, "value_in": value_in, "filt": filt, "gain": gain, "w_gate": w_gate, "w_up": w_up, "g_hid": g_hid, "g_res": g_res}


epsilon = 1e-06

def reference(resid_in, query_in, key_in, value_in, filt, gain, w_gate, w_up, g_hid, g_res):
    length = resid_in.shape[0]
    query_f = query_in.astype(jnp.float32)
    keys_f = key_in.astype(jnp.float32)
    values_f = value_in.astype(jnp.float32)
    mixed = (keys_f * values_f).astype(jnp.bfloat16)
    padded_len = 2 * length
    spec_src = jnp.fft.rfft(mixed.astype(jnp.float32), n=padded_len, axis=0)
    spec_filt = jnp.fft.rfft(filt.T, n=padded_len, axis=0)
    conv = jnp.fft.irfft(spec_src * spec_filt, n=padded_len, axis=0)[:length]
    conv_b = conv.astype(jnp.bfloat16)
    conv_f = conv_b.astype(jnp.float32)
    resid = resid_in.astype(jnp.float32) + query_f * conv_f
    inv_rms = lax.rsqrt(lax.optimization_barrier(jnp.sum(resid * resid, axis=1)) / D + epsilon)
    normed = resid * gain[None, :] * inv_rms[:, None]
    amax = jnp.max(jnp.abs(normed))
    acts = normed.astype(jnp.bfloat16)
    gate = jnp.dot(acts, w_gate, preferred_element_type=jnp.float32)
    up = jnp.dot(acts, w_up, preferred_element_type=jnp.float32)
    sigma = jax.nn.sigmoid(gate)
    hid_grad = g_hid.astype(jnp.float32)
    d_gate = (hid_grad * up * sigma * (1.0 + gate * (1.0 - sigma))).astype(jnp.bfloat16)
    d_up = (hid_grad * gate * sigma).astype(jnp.bfloat16)
    dw_gate = jnp.dot(acts.T, d_gate, preferred_element_type=jnp.float32)
    dw_up = jnp.dot(acts.T, d_up, preferred_element_type=jnp.float32)
    block = FF // N_CH

    def add_block(total, index):
        start = (index * block).astype(jnp.int32)
        gate_part = lax.dynamic_slice_in_dim(d_gate, start, block, 1)
        up_part = lax.dynamic_slice_in_dim(d_up, start, block, 1)
        wgate_part = lax.dynamic_slice_in_dim(w_gate, start, block, 1)
        wup_part = lax.dynamic_slice_in_dim(w_up, start, block, 1)
        term = jnp.dot(gate_part, wgate_part.T, preferred_element_type=jnp.float32)
        term = term + jnp.dot(up_part, wup_part.T, preferred_element_type=jnp.float32)
        rounded = lax.optimization_barrier(term.astype(jnp.bfloat16))
        return (total + rounded.astype(jnp.float32), None)
    d_norm, _ = lax.scan(add_block, jnp.zeros(resid_in.shape, jnp.float32), jnp.arange(N_CH, dtype=jnp.int32))
    dgain = lax.optimization_barrier(jnp.sum(d_norm * resid * inv_rms[:, None], axis=0))
    scaled_grad = gain[None, :] * d_norm
    inner = lax.optimization_barrier(jnp.sum(scaled_grad * resid, axis=1))
    d_resid = g_res.astype(jnp.float32) + scaled_grad * inv_rms[:, None] - resid * (inv_rms ** 3 * inner / D)[:, None]
    dx = d_resid.astype(jnp.bfloat16)
    dq = (d_resid * conv_f).astype(jnp.bfloat16)
    d_conv = (d_resid * query_f).astype(jnp.bfloat16)
    spec_grad = jnp.fft.rfft(d_conv.astype(jnp.float32), n=padded_len, axis=0)
    src_grad = jnp.fft.irfft(spec_grad * jnp.conj(spec_filt), n=padded_len, axis=0)[:length]
    src_grad = src_grad.astype(jnp.bfloat16).astype(jnp.float32)
    dk = (src_grad * values_f).astype(jnp.bfloat16)
    dv = (src_grad * keys_f).astype(jnp.bfloat16)
    dfilt = jnp.fft.irfft(spec_grad * jnp.conj(spec_src), n=padded_len, axis=0)[:length].T
    return (dx, dq, dk, dv, dfilt, dgain, dw_gate, dw_up, amax)
```

```python
import math

import jax
import jax.numpy as jnp
from jax import lax
from jax.sharding import PartitionSpec as P

epsilon = 1e-06
highest = lax.Precision.HIGHEST


def split_sizes(total):
    size_p = math.gcd(total, 2 ** (total.bit_length() // 2))
    return (size_p, total // size_p)


def dft_tables(size_p, size_q):
    total = size_p * size_q
    rows_p = jnp.arange(size_p, dtype=jnp.int32)
    rows_q = jnp.arange(size_q, dtype=jnp.int32)
    angle_p = (rows_p[:, None] * rows_p[None, :] % size_p).astype(jnp.float32) * (
        2.0 * math.pi / size_p
    )
    angle_q = (rows_q[:, None] * rows_q[None, :] % size_q).astype(jnp.float32) * (
        2.0 * math.pi / size_q
    )
    angle_t = (rows_p[:, None] * rows_q[None, :] % total).astype(jnp.float32) * (
        2.0 * math.pi / total
    )
    return (
        jnp.cos(angle_p),
        jnp.sin(angle_p),
        jnp.cos(angle_q),
        jnp.sin(angle_q),
        jnp.cos(angle_t),
        jnp.sin(angle_t),
    )


def left_mult(table, block):
    return jnp.einsum("kp,cpq->ckq", table, block, precision=highest)


def right_mult(block, table):
    return jnp.einsum("ckq,qm->ckm", block, table, precision=highest)


def forward_dft(signal, tables):
    cos_p, sin_p, cos_q, sin_q, cos_t, sin_t = tables
    chans = signal.shape[0]
    block = signal.reshape(chans, cos_p.shape[0], cos_q.shape[0])
    first_re = left_mult(cos_p, block)
    first_im = -left_mult(sin_p, block)
    turn_re = first_re * cos_t + first_im * sin_t
    turn_im = first_im * cos_t - first_re * sin_t
    out_re = right_mult(turn_re, cos_q) + right_mult(turn_im, sin_q)
    out_im = right_mult(turn_im, cos_q) - right_mult(turn_re, sin_q)
    return (out_re, out_im)


def inverse_dft(spec_re, spec_im, tables):
    cos_p, sin_p, cos_q, sin_q, cos_t, sin_t = tables
    chans = spec_re.shape[0]
    total = cos_p.shape[0] * cos_q.shape[0]
    mid_re = right_mult(spec_re, cos_q) - right_mult(spec_im, sin_q)
    mid_im = right_mult(spec_re, sin_q) + right_mult(spec_im, cos_q)
    turn_re = mid_re * cos_t - mid_im * sin_t
    turn_im = mid_re * sin_t + mid_im * cos_t
    signal = left_mult(cos_p, turn_re) - left_mult(sin_p, turn_im)
    return signal.reshape(chans, total) / total


def spectral_product(left_re, left_im, right_re, right_im, conjugate):
    if conjugate:
        return (left_re * right_re + left_im * right_im, left_im * right_re - left_re * right_im)
    return (left_re * right_re - left_im * right_im, left_re * right_im + left_im * right_re)


def padded(signal, length):
    return jnp.concatenate([signal, jnp.zeros((signal.shape[0], length), jnp.float32)], axis=1)


def gather_ch(block):
    copies = lax.axis_size("ch")
    spread = jnp.broadcast_to(block[None], (copies,) + block.shape)
    return lax.all_to_all(spread, "ch", split_axis=0, concat_axis=0, tiled=True)


def split_rows(row):
    high = lax.reduce_precision(row, 8, 7)
    rest = row - high
    mid = lax.reduce_precision(rest, 8, 7)
    low = rest - mid
    return jnp.stack([high, mid, low]).astype(jnp.bfloat16)


def join_rows(rows):
    rows = rows.astype(jnp.float32)
    return rows[..., 0, :] + rows[..., 1, :] + rows[..., 2, :]


def on_device(resid_in, query_in, key_in, value_in, filt, gain, w_gate, w_up, g_hid, g_res):
    tokens, chans = resid_in.shape
    n_ctx = lax.axis_size("ctx")
    n_ch = lax.axis_size("ch")
    length = tokens * n_ctx
    width = chans * n_ch
    rows, hidden = w_gate.shape
    lanes = -(-hidden // 128) * 128
    my_ch = lax.axis_index("ch")
    size_p, size_q = split_sizes(2 * length)
    tables = dft_tables(size_p, size_q)

    def widen(block):
        return jnp.pad(block, ((0, 0), (0, lanes - hidden)))

    w_all = lax.all_gather(
        jnp.concatenate([widen(w_gate), widen(w_up)], axis=1), "ctx", axis=0, tiled=True
    )
    query_f = query_in.T.astype(jnp.float32)
    keys_f = key_in.T.astype(jnp.float32)
    values_f = value_in.T.astype(jnp.float32)
    mixed = (keys_f * values_f).astype(jnp.bfloat16)
    spread = lax.all_to_all(mixed, "ctx", split_axis=0, concat_axis=1, tiled=True)
    src_re, src_im = forward_dft(padded(spread.astype(jnp.float32), length), tables)
    filt_re, filt_im = forward_dft(padded(filt, length), tables)
    conv_re, conv_im = spectral_product(src_re, src_im, filt_re, filt_im, False)
    conv_full = inverse_dft(conv_re, conv_im, tables)[:, :length].astype(jnp.bfloat16)
    conv_f = lax.all_to_all(conv_full, "ctx", split_axis=1, concat_axis=0, tiled=True).astype(
        jnp.float32
    )
    resid = resid_in.T.astype(jnp.float32) + query_f * conv_f
    scaled_res = resid * gain[:, None]
    payload = jnp.concatenate(
        [
            scaled_res.astype(jnp.bfloat16),
            split_rows(jnp.sum(resid * resid, axis=0)),
            jnp.zeros((5, tokens), jnp.bfloat16),
        ]
    )
    met = gather_ch(payload)
    acts = met[:, :chans].reshape(width, tokens)
    inv_rms = lax.rsqrt(jnp.sum(join_rows(met[:, chans : chans + 3]), axis=0) / width + epsilon)
    inv_col = inv_rms[:, None]
    amax = jnp.max(jnp.abs(scaled_res * inv_rms[None, :]))

    piece = lax.dynamic_slice_in_dim(acts.reshape(n_ctx, rows, tokens), my_ch * (rows // n_ch), rows // n_ch, 1)
    piece = lax.all_to_all(piece, "ctx", split_axis=0, concat_axis=0, tiled=True)
    piece = piece.transpose(1, 0, 2).reshape(rows // n_ch, length)
    row_acts = gather_ch(piece).reshape(rows, length)

    both = lax.dot_general(
        acts, w_all, (((0,), (0,)), ((), ())), preferred_element_type=jnp.float32
    )
    both = both * inv_col
    gate = both[:, :lanes]
    up = both[:, lanes:]
    sigma = jax.nn.sigmoid(gate)
    hid_grad = widen(g_hid).astype(jnp.float32)
    d_gate = hid_grad * up * sigma * (1.0 + gate * (1.0 - sigma))
    d_up = hid_grad * gate * sigma
    d_both = jnp.concatenate([d_gate, d_up], axis=1)
    inner_part = jnp.sum(d_both * both, axis=1)
    d_hid = d_both.astype(jnp.bfloat16)
    d_all = lax.all_gather((d_both * inv_col).astype(jnp.bfloat16), "ctx", axis=0, tiled=True)
    term = lax.dot_general(
        w_all, d_hid, (((1,), (1,)), ((), ())), preferred_element_type=jnp.float32
    )
    term = term.astype(jnp.bfloat16).reshape(n_ch, chans, tokens)
    extra = jnp.concatenate(
        [
            split_rows(inner_part),
            split_rows(jnp.full((tokens,), amax, jnp.float32)),
            jnp.zeros((2, tokens), jnp.bfloat16),
        ]
    )
    sent = jnp.concatenate([term, jnp.broadcast_to(extra[None], (n_ch, 8, tokens))], axis=1)
    back = lax.all_to_all(sent, "ch", split_axis=0, concat_axis=0, tiled=True)
    d_norm = jnp.sum(back[:, :chans].astype(jnp.float32), axis=0)
    inner = jnp.sum(join_rows(back[:, chans : chans + 3]), axis=0)
    amax = jnp.max(join_rows(back[:, chans + 3 : chans + 6]), axis=0)

    scaled_grad = gain[:, None] * d_norm
    gain_part = jnp.sum(d_norm * resid * inv_rms[None, :], axis=1)
    d_resid = (
        g_res.T.astype(jnp.float32)
        + scaled_grad * inv_rms[None, :]
        - resid * (inv_rms * inv_rms * inner / width)[None, :]
    )
    d_conv = (d_resid * query_f).astype(jnp.bfloat16)
    d_query = (d_resid * conv_f).astype(jnp.bfloat16)
    own = chans // n_ctx
    extra = jnp.concatenate([split_rows(gain_part), split_rows(amax), jnp.zeros((2, chans), jnp.bfloat16)])
    sent = jnp.concatenate(
        [d_conv.reshape(n_ctx, own, tokens), jnp.broadcast_to(extra[None], (n_ctx, 8, chans))], axis=1
    )
    back = lax.all_to_all(sent, "ctx", split_axis=0, concat_axis=0, tiled=True)
    gain_grad = jnp.sum(join_rows(back[:, own : own + 3]), axis=0)
    amax = jnp.max(join_rows(back[:, own + 3 : own + 6]))
    back_spread = back[:, :own].transpose(1, 0, 2).reshape(own, length)
    grad_re, grad_im = forward_dft(padded(back_spread.astype(jnp.float32), length), tables)
    srcg_re, srcg_im = spectral_product(grad_re, grad_im, filt_re, filt_im, True)
    src_grad = inverse_dft(srcg_re, srcg_im, tables)[:, :length].astype(jnp.bfloat16)
    fltg_re, fltg_im = spectral_product(grad_re, grad_im, src_re, src_im, True)
    filt_grad = inverse_dft(fltg_re, fltg_im, tables)[:, :length]
    src_tok = lax.all_to_all(src_grad, "ctx", split_axis=1, concat_axis=0, tiled=True).astype(
        jnp.float32
    )
    d_keys = (src_tok * values_f).astype(jnp.bfloat16)
    d_values = (src_tok * keys_f).astype(jnp.bfloat16)
    first = jnp.dot(row_acts, d_all[:, :lanes], preferred_element_type=jnp.float32)
    second = jnp.dot(row_acts, d_all[:, lanes:], preferred_element_type=jnp.float32)
    return (
        d_resid.astype(jnp.bfloat16).T,
        d_query.T,
        d_keys.T,
        d_values.T,
        filt_grad,
        gain_grad,
        first[:, :hidden],
        second[:, :hidden],
        amax,
    )


def solution(mesh):
    return jax.shard_map(
        on_device,
        mesh=mesh,
        in_specs=(
            P("ctx", "ch"),
            P("ctx", "ch"),
            P("ctx", "ch"),
            P("ctx", "ch"),
            P(("ch", "ctx"), None),
            P("ch"),
            P("ctx", "ch"),
            P("ctx", "ch"),
            P("ctx", "ch"),
            P("ctx", "ch"),
        ),
        out_specs=(
            P("ctx", "ch"),
            P("ctx", "ch"),
            P("ctx", "ch"),
            P("ctx", "ch"),
            P(("ch", "ctx"), None),
            P("ch"),
            P("ctx", "ch"),
            P("ctx", "ch"),
            P(),
        ),
        check_vma=False,
    )
```

```python
import functools
import math

import jax
import jax.numpy as jnp
import numpy as np
from jax import lax
from jax.experimental import pallas as pl
from jax.experimental.pallas import tpu as pltpu
from jax.sharding import PartitionSpec as P

epsilon = 1e-06
f32 = jnp.float32
bf16 = jnp.bfloat16
VMEM = pl.BlockSpec(memory_space=pltpu.VMEM)
HBM = pl.BlockSpec(memory_space=pltpu.HBM)
EXTRA = 16


def call(body, outs, n_in, flops=1e8, in_specs=None, out_specs=None, scratch=(), limit=8, hbm=(), vmem=()):
    return pl.pallas_call(
        body,
        out_shape=tuple(
            pltpu.HBM(s, d) if k in hbm else pltpu.VMEM(s, d) if k in vmem else jax.ShapeDtypeStruct(s, d)
            for k, (s, d) in enumerate(outs)
        ),
        in_specs=in_specs or [VMEM] * n_in,
        out_specs=tuple(out_specs or [VMEM] * len(outs)),
        scratch_shapes=list(scratch),
        compiler_params=pltpu.CompilerParams(vmem_limit_bytes=limit * 2**20),
        cost_estimate=pl.CostEstimate(flops=int(flops), bytes_accessed=2**20, transcendentals=0),
    )


def split_table(table):
    high = table.astype(np.float32).astype(jnp.bfloat16)
    low = (table - high.astype(np.float64)).astype(np.float32).astype(jnp.bfloat16)
    return np.asarray(high), np.asarray(low)


@functools.cache
def dft_tables(blocks, chans, lanes):
    turns = 2 * blocks
    half = blocks + 1
    total = turns * lanes
    freq = np.arange(half)
    eye = np.eye(chans)
    angle = 2.0 * np.pi * (np.outer(freq, np.arange(blocks)) % turns) / turns
    first = np.concatenate([np.kron(np.cos(angle), eye), np.kron(-np.sin(angle), eye)])
    weight = np.where((freq == 0) | (freq == blocks), 1.0, 2.0)[:, None] / total
    last = np.concatenate(
        [np.kron(weight * np.cos(angle), eye), np.kron(-weight * np.sin(angle), eye)]
    ).T
    angle = 2.0 * np.pi * (np.outer(np.arange(lanes), np.arange(lanes)) % lanes) / lanes
    inner = np.concatenate([np.cos(angle), np.sin(angle)], axis=1)
    angle = 2.0 * np.pi * np.repeat(np.outer(freq, np.arange(lanes)), chans, axis=0) / total
    twiddle = np.stack([np.cos(angle), np.sin(angle)]).astype(np.float32)
    last = np.pad(last, ((0, 0), (0, -last.shape[1] % lanes)))
    wide = [np.concatenate(np.split(t, t.shape[1] // lanes, axis=1)) for t in (last, inner)]
    return (*split_table(first), *split_table(wide[0]), *split_table(wide[1]), twiddle)


def read_tables(refs):
    tables = []
    for ref in refs:
        table = ref[...]
        if 2 <= len(tables) < 6:
            lanes = table.shape[1]
            table = jnp.concatenate(
                [table[k : k + lanes] for k in range(0, table.shape[0], lanes)], axis=1
            )
        tables.append(table)
    return tables


def pair(value):
    high = value.astype(bf16)
    return high, (value - high.astype(f32)).astype(bf16)


def dot(left, right):
    return jnp.dot(left, right, preferred_element_type=f32)


def turn_lanes(parts, inner_hi, inner_lo, lanes, sign):
    rows = parts.shape[0] // 2
    high, low = pair(parts)
    both = dot(high, inner_hi) + (dot(high, inner_lo) + dot(low, inner_hi))
    by_cos, by_sin = both[:, :lanes], both[:, lanes:]
    real = by_cos[:rows] - sign * by_sin[rows:]
    imag = by_cos[rows:] + sign * by_sin[:rows]
    return real, imag


def to_spectrum(signal, tables, exact):
    first_hi, first_lo, _, _, inner_hi, inner_lo, twiddle = tables
    lanes = signal.shape[1]
    if exact:
        signal = signal.astype(bf16)
        out = dot(first_hi, signal) + dot(first_lo, signal)
    else:
        high, low = pair(signal)
        out = dot(first_hi, high) + (dot(first_hi, low) + dot(first_lo, high))
    rows = out.shape[0] // 2
    real, imag = out[:rows], out[rows:]
    cos, sin = twiddle[0], twiddle[1]
    turned = jnp.concatenate([real * cos + imag * sin, imag * cos - real * sin])
    return turn_lanes(turned, inner_hi, inner_lo, lanes, -1.0)


def from_spectrum(real, imag, tables):
    _, _, last_hi, last_lo, inner_hi, inner_lo, twiddle = tables
    lanes = real.shape[1]
    real, imag = turn_lanes(jnp.concatenate([real, imag]), inner_hi, inner_lo, lanes, 1.0)
    cos, sin = twiddle[0], twiddle[1]
    both = jnp.concatenate([real * cos - imag * sin, real * sin + imag * cos])
    rest = jnp.zeros((last_hi.shape[1] - both.shape[0], lanes), f32)
    high, low = pair(jnp.concatenate([both, rest]))
    return dot(last_hi, high) + (dot(last_hi, low) + dot(last_lo, high))


def split_rows(row):
    high = row.astype(bf16).astype(f32)
    rest = row - high
    mid = rest.astype(bf16).astype(f32)
    low = rest - mid
    return [high, mid, low]


def start_kernel(key_ref, value_ref, resid_ref, query_ref, gate_ref, up_ref, sent_ref, w_ref):
    w_ref[0] = gate_ref[...]
    w_ref[1] = up_ref[...]
    n_ctx = sent_ref.shape[0]
    own = key_ref.shape[1] // n_ctx
    mixed = (key_ref[...].astype(f32) * value_ref[...].astype(f32)).astype(bf16)
    parts = [mixed.astype(f32).T, resid_ref[...].astype(f32).T, query_ref[...].astype(f32).T]
    for peer in range(n_ctx):
        rows = slice(peer * own, (peer + 1) * own)
        sent_ref[peer] = jnp.concatenate([part[rows] for part in parts]).astype(bf16)


def filter_kernel(filt_ref, *refs):
    n_kept = (len(refs) - 2) // 2
    kept, (re_ref, im_ref), copies = refs[:n_kept], refs[n_kept : n_kept + 2], refs[n_kept + 2 :]
    for source, copy in zip(kept, copies):
        copy[...] = source[...]
    tables = read_tables(kept[:7])
    lanes = kept[0].shape[1]
    blocks = filt_ref.shape[1] // lanes
    signal = jnp.concatenate([filt_ref[:, a * lanes : (a + 1) * lanes] for a in range(blocks)])
    re_ref[...], im_ref[...] = to_spectrum(signal, tables, False)


def conv_kernel(met_ref, gain_ref, fre_ref, fim_ref, *refs):
    tables = read_tables(refs[:7])
    conv_ref, sre_ref, sim_ref, piece_ref = refs[7:]
    n_ctx = met_ref.shape[0]
    own = conv_ref.shape[0] // n_ctx
    blocks = [met_ref[k].astype(f32) for k in range(n_ctx)]
    source, resid, query = (
        jnp.concatenate([block[p * own : (p + 1) * own] for block in blocks]) for p in range(3)
    )
    real, imag = to_spectrum(source, tables, True)
    sre_ref[...], sim_ref[...] = real, imag
    fre, fim = fre_ref[...], fim_ref[...]
    conv = from_spectrum(real * fre - imag * fim, real * fim + imag * fre, tables).astype(bf16)
    conv_ref[...] = conv
    piece_ref[...] = ((resid + query * conv.astype(f32)) * gain_ref[...]).astype(bf16)


def resid_kernel(conv_ref, resid_ref, query_ref, gain_ref, piece_ref, sent_ref, r_ref):
    chans, tokens = conv_ref.shape
    resid = resid_ref[...].astype(f32).T + query_ref[...].astype(f32).T * conv_ref[...].astype(f32)
    r_ref[...] = resid
    scaled = (resid * gain_ref[...]).astype(bf16)
    square = jnp.sum(resid * resid, axis=0, keepdims=True)
    extra = jnp.concatenate(split_rows(square) + [jnp.zeros((EXTRA - 3, tokens), f32)]).astype(bf16)
    piece = piece_ref[...]
    for peer in range(sent_ref.shape[0]):
        sent_ref[peer, :chans] = scaled
        sent_ref[peer, chans : chans + EXTRA] = extra
        sent_ref[peer, chans + EXTRA :] = piece


def load_weights(w_ref, w_vmem, sems):
    copies = [
        pltpu.make_async_copy(w_ref.at[i], w_vmem.at[i], sems.at[i]) for i in range(w_ref.shape[0])
    ]
    for copy in copies:
        copy.start()
    return copies


def hidden_kernel(
    met_ref, w_ref, grad_ref, r_ref, gain_ref, d_ref, hid_ref, inv_ref, extra_ref, w_vmem, sems
):
    copies = load_weights(w_ref, w_vmem, sems)
    n_ch, _, tokens = met_ref.shape
    chans = r_ref.shape[0]
    per = w_ref.shape[3] // chans
    total = jnp.zeros((8, tokens), f32)
    for peer in range(n_ch):
        total = total + met_ref[peer, chans : chans + EXTRA].astype(f32)[:8]
    inv = lax.rsqrt((total[0:1] + total[1:2] + total[2:3]) / (n_ch * chans) + epsilon)
    inv_ref[...] = inv
    amax = jnp.max(jnp.abs((r_ref[...] * gain_ref[...]) * inv), axis=0, keepdims=True)
    amax = jnp.max(amax, axis=1, keepdims=True)
    gate, up = None, None
    for i, copy in enumerate(copies):
        copy.wait()
        acts = jnp.concatenate([met_ref[i * per + k, :chans] for k in range(per)])
        part = dot(w_vmem[i, 0], acts)
        gate = part if gate is None else gate + part
        part = dot(w_vmem[i, 1], acts)
        up = part if up is None else up + part
    gate, up = gate * inv, up * inv
    sigma = 1.0 / (1.0 + jnp.exp(-gate))
    hid = grad_ref[...].astype(f32)
    d_gate = hid * up * sigma * (1.0 + gate * (1.0 - sigma))
    d_up = hid * gate * sigma
    d_ref[0] = (d_gate * inv).astype(bf16)
    d_ref[1] = (d_up * inv).astype(bf16)
    hid_ref[0] = d_gate.astype(bf16)
    hid_ref[1] = d_up.astype(bf16)
    inner = jnp.sum(d_gate * gate + d_up * up, axis=0, keepdims=True)
    extra_ref[...] = jnp.concatenate(
        split_rows(inner)
        + split_rows(jnp.broadcast_to(amax, (1, tokens)))
        + [jnp.zeros((EXTRA - 6, tokens), f32)]
    ).astype(bf16)


def back_kernel(w_ref, hid_ref, extra_ref, sent_ref, w_vmem, sent_vmem, sems, sent_sems):
    arrivals = load_weights(w_ref, w_vmem, sems)
    n_ch, padded, chans = sent_ref.shape
    tokens = padded - EXTRA
    per = w_ref.shape[3] // chans
    extra = extra_ref[...]
    parts = sent_sems.shape[0]
    share = n_ch // parts
    copies = []
    for i, arrival in enumerate(arrivals):
        arrival.wait()
        term = 0.0
        for half in range(2):
            term = term + lax.dot_general(
                hid_ref[half],
                w_vmem[i, half],
                (((0,), (0,)), ((), ())),
                preferred_element_type=f32,
            )
        term = term.astype(bf16)
        for k in range(per):
            sent_vmem[i * per + k, :tokens] = term[:, k * chans : (k + 1) * chans]
            sent_vmem[i * per + k, tokens:] = extra
        done = (i + 1) * per
        if done % share == 0:
            copy = pltpu.make_async_copy(
                sent_vmem.at[done - share : done],
                sent_ref.at[done - share : done],
                sent_sems.at[done // share - 1],
            )
            copy.start()
            copies.append(copy)
    for copy in copies:
        copy.wait()


def norm_kernel(
    back_ref, r_ref, conv_ref, query_ref, gres_ref, gain_ref, inv_ref, dx_ref, dq_ref, sent_ref
):
    n_ch = back_ref.shape[0]
    chans, tokens = r_ref.shape
    n_ctx = sent_ref.shape[0]
    own = chans // n_ctx
    total = back_ref[0, :tokens].astype(f32)
    extra = back_ref[0, tokens : tokens + EXTRA].astype(f32)[:8]
    inner, peak = extra[0:1] + extra[1:2] + extra[2:3], extra[3:4] + extra[4:5] + extra[5:6]
    for peer in range(1, n_ch):
        total = total + back_ref[peer, :tokens].astype(f32)
        extra = back_ref[peer, tokens : tokens + EXTRA].astype(f32)[:8]
        inner = inner + (extra[0:1] + extra[1:2] + extra[2:3])
        peak = jnp.maximum(peak, extra[3:4] + extra[4:5] + extra[5:6])
    d_norm = total.T
    resid = r_ref[...]
    inv = inv_ref[...]
    gain = gain_ref[...]
    d_resid = (
        gres_ref[...].astype(f32).T
        + (gain * d_norm) * inv
        - resid * (inv * inv * inner / (n_ch * chans))
    )
    dx_ref[...] = d_resid.T.astype(bf16)
    dq_ref[...] = (d_resid * conv_ref[...].astype(f32)).T.astype(bf16)
    d_conv = (d_resid * query_ref[...].astype(f32).T).astype(bf16).astype(f32)
    product = (d_norm * resid * inv).T
    gain_part = jnp.sum(product, axis=0, keepdims=True)
    extra = split_rows(gain_part) + split_rows(peak) + [jnp.zeros((2, chans), f32)]
    for peer in range(n_ctx):
        rows = slice(peer * own, (peer + 1) * own)
        sent_ref[peer] = jnp.concatenate([d_conv[rows]] + extra).astype(bf16)


def rows_kernel(back_ref, out_ref):
    n_ch = back_ref.shape[0]
    lanes = back_ref.shape[2]
    start = back_ref.shape[1] - lanes
    blocks = out_ref.shape[1] // lanes
    own = lanes // blocks
    pair_of = EXTRA // own
    for first in range(0, n_ch, pair_of):
        parts = []
        for peer in range(first, first + pair_of):
            block = back_ref[peer, start:].astype(f32)
            parts.append(
                jnp.concatenate([block[a * own : (a + 1) * own] for a in range(blocks)], axis=1)
            )
        out_ref[first * own : (first + pair_of) * own] = jnp.concatenate(parts).astype(bf16)


def grad_kernel(back_ref, fre_ref, fim_ref, *refs):
    tables = read_tables(refs[:7])
    ds_ref, gre_ref, gim_ref, dgain_ref, amax_ref = refs[7:]
    n_ctx = back_ref.shape[0]
    own = ds_ref.shape[0] // n_ctx
    blocks = [back_ref[k].astype(f32) for k in range(n_ctx)]
    real, imag = to_spectrum(jnp.concatenate([b[:own] for b in blocks]), tables, True)
    gre_ref[...], gim_ref[...] = real, imag
    fre, fim = fre_ref[...], fim_ref[...]
    back = from_spectrum(real * fre + imag * fim, imag * fre - real * fim, tables)
    ds_ref[...] = back.astype(bf16)
    gain, peak = None, None
    for block in blocks:
        extra = block[own:]
        g = extra[0:1] + extra[1:2] + extra[2:3]
        p = extra[3:4] + extra[4:5] + extra[5:6]
        gain = g if gain is None else gain + g
        peak = p if peak is None else jnp.maximum(peak, p)
    dgain_ref[...] = gain
    amax_ref[...] = jnp.max(peak, axis=1, keepdims=True)


def filter_grad_kernel(gre_ref, gim_ref, sre_ref, sim_ref, *refs):
    tables = read_tables(refs[:7])
    out_ref = refs[7]
    own = out_ref.shape[0]
    real, imag, sre, sim = gre_ref[...], gim_ref[...], sre_ref[...], sim_ref[...]
    grad = from_spectrum(real * sre + imag * sim, imag * sre - real * sim, tables)
    lanes = grad.shape[1]
    for a in range(out_ref.shape[1] // lanes):
        out_ref[:, a * lanes : (a + 1) * lanes] = grad[a * own : (a + 1) * own]


def products_kernel(ds_ref, key_ref, value_ref, dk_ref, dv_ref):
    grad = ds_ref[...].astype(f32).T
    dk_ref[...] = (grad * value_ref[...].astype(f32)).astype(bf16)
    dv_ref[...] = (grad * key_ref[...].astype(f32)).astype(bf16)


def weight_kernel(d_ref, rows_ref, first_ref, second_ref, d_vmem, sems):
    n_ctx, _, _, tokens = d_ref.shape
    copies = load_weights(d_ref, d_vmem, sems)
    acc = [0.0, 0.0]
    for i in range(n_ctx):
        copies[i].wait()
        for half in range(2):
            acc[half] = acc[half] + lax.dot_general(
                d_vmem[i, half],
                rows_ref[:, i * tokens : (i + 1) * tokens],
                (((1,), (1,)), ((), ())),
                preferred_element_type=f32,
            )
    first_ref[...] = acc[0]
    second_ref[...] = acc[1]


def on_device(resid_in, query_in, key_in, value_in, filt, gain, w_gate, w_up, g_hid, g_res):
    tokens, chans = resid_in.shape
    n_ctx = lax.axis_size("ctx")
    n_ch = lax.axis_size("ch")
    length = tokens * n_ctx
    rows, hidden = w_gate.shape
    own = chans // n_ctx
    tables = dft_tables(n_ctx, own, tokens)
    spec_rows = tables[6].shape[1]

    def in_hbm(array):
        return pltpu.with_memory_space_constraint(array, pltpu.HBM)

    tables = [in_hbm(jnp.asarray(table)) for table in tables]
    key_in, value_in, resid_in, query_in, g_res, filt = (
        in_hbm(array) for array in (key_in, value_in, resid_in, query_in, g_res, filt)
    )
    spectrum = ((spec_rows, tokens), f32)
    square = ((chans, tokens), bf16)
    gain_col = gain[:, None]
    gain_own = jnp.tile(
        lax.dynamic_slice_in_dim(gain_col, lax.axis_index("ctx") * own, own, 0), (n_ctx, 1)
    )
    groups = 4

    weights_vmem = pltpu.VMEM((n_ctx, 2, hidden, rows), bf16)
    weights_sems = pltpu.SemaphoreType.DMA((n_ctx,))
    places = []
    for i in range(n_ctx):
        for j in range(n_ch):
            block = i * n_ch + j
            held_by = (block % n_ctx) * n_ch + block // n_ctx
            places.append((held_by, block))

    sent, w_both = call(
        start_kernel,
        [((n_ctx, 3 * own, tokens), bf16), ((2, hidden, rows), bf16)],
        6,
        hbm=(0, 1),
    )(key_in, value_in, resid_in, query_in, in_hbm(w_gate.T), in_hbm(w_up.T))
    w_all = in_hbm(lax.all_gather(w_both, "ctx", axis=0, tiled=False))
    met = lax.all_to_all(sent, "ctx", 0, 0, tiled=True)
    kept = [*tables, key_in, value_in, resid_in, query_in, g_res]
    fre, fim, *kept = call(
        filter_kernel,
        [spectrum] * 2 + [(array.shape, array.dtype) for array in kept],
        len(kept) + 1,
        vmem=range(len(kept) + 2),
    )(filt, *kept)
    tables = kept[:7]
    key_in, value_in, resid_in, query_in, g_res = kept[7:]
    conv, sre, sim, piece = call(conv_kernel, [square, spectrum, spectrum, square], 11, vmem=(1, 2))(
        met, gain_own, fre, fim, *tables
    )
    piece = lax.ppermute(piece, ("ctx", "ch"), places)
    conv = lax.all_to_all(conv.reshape(n_ctx, own, tokens), "ctx", 0, 0, tiled=True).reshape(
        chans, tokens
    )
    sent, resid = call(
        resid_kernel,
        [((n_ch, 2 * chans + EXTRA, tokens), bf16), ((chans, tokens), f32)],
        5,
    )(conv, resid_in, query_in, gain_col, piece)
    met = lax.all_to_all(sent, "ch", 0, 0, tiled=True)
    (row_acts,) = call(rows_kernel, [((rows, length), bf16)], 1)(met)
    d_scaled, d_hid, inv, extra = call(
        hidden_kernel,
        [
            ((2, hidden, tokens), bf16),
            ((2, hidden, tokens), bf16),
            ((1, tokens), f32),
            ((EXTRA, tokens), bf16),
        ],
        5,
        in_specs=[VMEM, HBM, VMEM, VMEM, VMEM],
        scratch=[weights_vmem, weights_sems],
        flops=1e9,
        limit=16,
    )(met, w_all, in_hbm(g_hid.T), resid, gain_col)
    d_all = in_hbm(lax.all_gather(d_scaled, "ctx", axis=0, tiled=False))
    sent_shape = (n_ch, tokens + EXTRA, chans)
    (sent,) = call(
        back_kernel,
        [(sent_shape, bf16)],
        3,
        in_specs=[HBM, VMEM, VMEM],
        out_specs=[HBM],
        scratch=[
            weights_vmem,
            pltpu.VMEM(sent_shape, bf16),
            weights_sems,
            pltpu.SemaphoreType.DMA((groups,)),
        ],
        flops=1e9,
        limit=16,
    )(w_all, d_hid, extra)
    back = lax.all_to_all(sent, "ch", 0, 0, tiled=True)
    dx, dq, sent = call(
        norm_kernel,
        [((tokens, chans), bf16), ((tokens, chans), bf16), ((n_ctx, 2 * own, tokens), bf16)],
        7,
    )(back, resid, conv, query_in, g_res, gain_col, inv)
    back = lax.all_to_all(sent, "ctx", 0, 0, tiled=True)
    ds, gre, gim, dgain, amax = call(
        grad_kernel,
        [square, spectrum, spectrum, ((1, chans), f32), ((1, 1), f32)],
        10,
        vmem=(1, 2),
    )(back, fre, fim, *tables)
    ds = lax.all_to_all(ds.reshape(n_ctx, own, tokens), "ctx", 0, 0, tiled=True)
    (dfilt,) = call(filter_grad_kernel, [(filt.shape, f32)], 11)(gre, gim, sre, sim, *tables)
    dk, dv = call(products_kernel, [((tokens, chans), bf16)] * 2, 3)(
        ds.reshape(chans, tokens), key_in, value_in
    )
    first, second = call(
        weight_kernel,
        [((hidden, rows), f32)] * 2,
        2,
        in_specs=[HBM, VMEM],
        scratch=[pltpu.VMEM((n_ctx, 2, hidden, tokens), bf16), pltpu.SemaphoreType.DMA((n_ctx,))],
        flops=1e9,
        limit=16,
    )(d_all, row_acts)
    return (dx, dq, dk, dv, dfilt, dgain[0], first.T, second.T, amax[0, 0])


def solution(mesh):
    return jax.shard_map(
        on_device,
        mesh=mesh,
        in_specs=(
            P("ctx", "ch"),
            P("ctx", "ch"),
            P("ctx", "ch"),
            P("ctx", "ch"),
            P(("ch", "ctx"), None),
            P("ch"),
            P("ctx", "ch"),
            P("ctx", "ch"),
            P("ctx", "ch"),
            P("ctx", "ch"),
        ),
        out_specs=(
            P("ctx", "ch"),
            P("ctx", "ch"),
            P("ctx", "ch"),
            P("ctx", "ch"),
            P(("ch", "ctx"), None),
            P("ch"),
            P("ctx", "ch"),
            P("ctx", "ch"),
            P(),
        ),
        check_vma=False,
    )
```

```python
import functools
import math

import jax
import jax.numpy as jnp
import numpy as np
from jax import lax
from jax.experimental import pallas as pl
from jax.experimental.pallas import tpu as pltpu
from jax.sharding import PartitionSpec as P

epsilon = 1e-06
f32 = jnp.float32
bf16 = jnp.bfloat16
VMEM = pl.BlockSpec(memory_space=pltpu.VMEM)
HBM = pl.BlockSpec(memory_space=pltpu.HBM)
EXTRA = 16


def call(body, outs, n_in, flops=1e8, in_specs=None, out_specs=None, scratch=(), limit=8, hbm=(), vmem=()):
    return pl.pallas_call(
        body,
        out_shape=tuple(
            pltpu.HBM(s, d) if k in hbm else pltpu.VMEM(s, d) if k in vmem else jax.ShapeDtypeStruct(s, d)
            for k, (s, d) in enumerate(outs)
        ),
        in_specs=in_specs or [VMEM] * n_in,
        out_specs=tuple(out_specs or [VMEM] * len(outs)),
        scratch_shapes=list(scratch),
        compiler_params=pltpu.CompilerParams(vmem_limit_bytes=limit * 2**20),
        cost_estimate=pl.CostEstimate(flops=int(flops), bytes_accessed=2**20, transcendentals=0),
    )


def split_table(table):
    high = table.astype(np.float32).astype(jnp.bfloat16)
    low = (table - high.astype(np.float64)).astype(np.float32).astype(jnp.bfloat16)
    return np.asarray(high), np.asarray(low)


@functools.cache
def dft_tables(blocks, chans, lanes):
    turns = 2 * blocks
    half = blocks + 1
    total = turns * lanes
    freq = np.arange(half)
    eye = np.eye(chans)
    angle = 2.0 * np.pi * (np.outer(freq, np.arange(blocks)) % turns) / turns
    first = np.concatenate([np.kron(np.cos(angle), eye), np.kron(-np.sin(angle), eye)])
    weight = np.where((freq == 0) | (freq == blocks), 1.0, 2.0)[:, None] / total
    last = np.concatenate(
        [np.kron(weight * np.cos(angle), eye), np.kron(-weight * np.sin(angle), eye)]
    ).T
    angle = 2.0 * np.pi * (np.outer(np.arange(lanes), np.arange(lanes)) % lanes) / lanes
    inner = np.concatenate([np.cos(angle), np.sin(angle)], axis=1)
    angle = 2.0 * np.pi * np.repeat(np.outer(freq, np.arange(lanes)), chans, axis=0) / total
    twiddle = np.stack([np.cos(angle), np.sin(angle)]).astype(np.float32)
    last = np.pad(last, ((0, 0), (0, -last.shape[1] % lanes)))
    wide = [np.concatenate(np.split(t, t.shape[1] // lanes, axis=1)) for t in (last, inner)]
    return (*split_table(first), *split_table(wide[0]), *split_table(wide[1]), twiddle)


def read_tables(refs):
    tables = []
    for ref in refs:
        table = ref[...]
        if 2 <= len(tables) < 6:
            lanes = table.shape[1]
            table = jnp.concatenate(
                [table[k : k + lanes] for k in range(0, table.shape[0], lanes)], axis=1
            )
        tables.append(table)
    return tables


def pair(value):
    high = value.astype(bf16)
    return high, (value - high.astype(f32)).astype(bf16)


def dot(left, right):
    return jnp.dot(left, right, preferred_element_type=f32)


def turn_lanes(parts, inner_hi, inner_lo, lanes, sign):
    rows = parts.shape[0] // 2
    high, low = pair(parts)
    both = dot(high, inner_hi) + (dot(high, inner_lo) + dot(low, inner_hi))
    by_cos, by_sin = both[:, :lanes], both[:, lanes:]
    real = by_cos[:rows] - sign * by_sin[rows:]
    imag = by_cos[rows:] + sign * by_sin[:rows]
    return real, imag


def to_spectrum(signal, tables, exact):
    first_hi, first_lo, _, _, inner_hi, inner_lo, twiddle = tables
    lanes = signal.shape[1]
    if exact:
        signal = signal.astype(bf16)
        out = dot(first_hi, signal) + dot(first_lo, signal)
    else:
        high, low = pair(signal)
        out = dot(first_hi, high) + (dot(first_hi, low) + dot(first_lo, high))
    rows = out.shape[0] // 2
    real, imag = out[:rows], out[rows:]
    cos, sin = twiddle[0], twiddle[1]
    turned = jnp.concatenate([real * cos + imag * sin, imag * cos - real * sin])
    return turn_lanes(turned, inner_hi, inner_lo, lanes, -1.0)


def from_spectrum(real, imag, tables):
    _, _, last_hi, last_lo, inner_hi, inner_lo, twiddle = tables
    lanes = real.shape[1]
    real, imag = turn_lanes(jnp.concatenate([real, imag]), inner_hi, inner_lo, lanes, 1.0)
    cos, sin = twiddle[0], twiddle[1]
    both = jnp.concatenate([real * cos - imag * sin, real * sin + imag * cos])
    rest = jnp.zeros((last_hi.shape[1] - both.shape[0], lanes), f32)
    high, low = pair(jnp.concatenate([both, rest]))
    return dot(last_hi, high) + (dot(last_hi, low) + dot(last_lo, high))


def split_rows(row):
    high = row.astype(bf16).astype(f32)
    rest = row - high
    mid = rest.astype(bf16).astype(f32)
    low = rest - mid
    return [high, mid, low]


def start_kernel(key_ref, value_ref, gate_ref, up_ref, mixed_ref, w_ref):
    w_ref[0] = gate_ref[...]
    w_ref[1] = up_ref[...]
    mixed = (key_ref[...].astype(f32) * value_ref[...].astype(f32)).astype(bf16)
    mixed_ref[...] = mixed.astype(f32).T.astype(bf16)


def reload_kernel(mark_ref, *refs):
    half = len(refs) // 2
    for source, copy in zip(refs[:half], refs[half:]):
        copy[...] = source[...]


def filter_kernel(filt_ref, *refs):
    n_kept = (len(refs) - 4) // 2
    kept, spectra, copies = refs[:n_kept], refs[n_kept : n_kept + 4], refs[n_kept + 4 :]
    for source, copy in zip(kept, copies):
        copy[...] = source[...]
    tables = read_tables(kept[:7])
    lanes = kept[0].shape[1]
    blocks = filt_ref.shape[1] // lanes
    signal = jnp.concatenate([filt_ref[:, a * lanes : (a + 1) * lanes] for a in range(blocks)])
    real, imag = to_spectrum(signal, tables, False)
    for k in range(2):
        spectra[2 * k][...], spectra[2 * k + 1][...] = real, imag


def conv_kernel(src_ref, fre_ref, fim_ref, *refs):
    tables = read_tables(refs[:7])
    conv_ref, sre_ref, sim_ref = refs[7:]
    real, imag = to_spectrum(src_ref[...], tables, True)
    sre_ref[...], sim_ref[...] = real, imag
    fre, fim = fre_ref[...], fim_ref[...]
    conv = from_spectrum(real * fre - imag * fim, real * fim + imag * fre, tables)
    conv_ref[...] = conv.astype(bf16)


def resid_kernel(conv_ref, resid_ref, query_ref, gain_ref, sent_ref, r_ref):
    chans, tokens = conv_ref.shape
    resid = resid_ref[...].astype(f32).T + query_ref[...].astype(f32).T * conv_ref[...].astype(f32)
    r_ref[...] = resid
    scaled = (resid * gain_ref[...]).astype(bf16)
    square = jnp.sum(resid * resid, axis=0, keepdims=True)
    extra = jnp.concatenate(split_rows(square) + [jnp.zeros((EXTRA - 3, tokens), f32)]).astype(bf16)
    for peer in range(sent_ref.shape[0]):
        sent_ref[peer, :chans] = scaled
        sent_ref[peer, chans:] = extra


def load_weights(w_ref, w_vmem, sems):
    copies = [
        pltpu.make_async_copy(w_ref.at[i], w_vmem.at[i], sems.at[i]) for i in range(w_ref.shape[0])
    ]
    for copy in copies:
        copy.start()
    return copies


def hidden_kernel(
    met_ref, w_ref, grad_ref, r_ref, gain_ref, d_ref, hid_ref, inv_ref, extra_ref, w_vmem, grad_vmem, sems, grad_sem
):
    copies = load_weights(w_ref, w_vmem, sems)
    grad_copy = pltpu.make_async_copy(grad_ref, grad_vmem, grad_sem)
    grad_copy.start()
    n_ch, _, tokens = met_ref.shape
    chans = r_ref.shape[0]
    per = w_ref.shape[3] // chans
    total = jnp.zeros((8, tokens), f32)
    for peer in range(n_ch):
        total = total + met_ref[peer, chans : chans + EXTRA].astype(f32)[:8]
    inv = lax.rsqrt((total[0:1] + total[1:2] + total[2:3]) / (n_ch * chans) + epsilon)
    inv_ref[...] = inv
    amax = jnp.max(jnp.abs((r_ref[...] * gain_ref[...]) * inv), axis=0, keepdims=True)
    amax = jnp.max(amax, axis=1, keepdims=True)
    gate, up = None, None
    for i, copy in enumerate(copies):
        copy.wait()
        acts = jnp.concatenate([met_ref[i * per + k, :chans] for k in range(per)])
        part = dot(w_vmem[i, 0], acts)
        gate = part if gate is None else gate + part
        part = dot(w_vmem[i, 1], acts)
        up = part if up is None else up + part
    gate, up = gate * inv, up * inv
    sigma = 1.0 / (1.0 + jnp.exp(-gate))
    grad_copy.wait()
    hid = grad_vmem[...].astype(f32)
    d_gate = hid * up * sigma * (1.0 + gate * (1.0 - sigma))
    d_up = hid * gate * sigma
    d_ref[0] = (d_gate * inv).astype(bf16)
    d_ref[1] = (d_up * inv).astype(bf16)
    rest = jnp.zeros((hid_ref.shape[2] - d_gate.shape[0], tokens), f32)
    for half, part in enumerate((d_gate, d_up)):
        hid_ref[half] = jnp.concatenate([part, rest]).T.astype(bf16)
    inner = jnp.sum(d_gate * gate + d_up * up, axis=0, keepdims=True)
    extra_ref[...] = jnp.concatenate(
        split_rows(inner)
        + split_rows(jnp.broadcast_to(amax, (1, tokens)))
        + [jnp.zeros((EXTRA - 6, tokens), f32)]
    ).astype(bf16)


def back_kernel(w_ref, hid_ref, extra_ref, sent_ref, w_vmem, sems):
    arrivals = load_weights(w_ref, w_vmem, sems)
    tokens = hid_ref.shape[1]
    cores, _, chans = sent_ref.shape
    n_ctx, _, hidden, rows = w_ref.shape
    per = rows // chans
    terms = n_ctx * per // cores * tokens
    for core in range(cores):
        sent_ref[core, terms:] = extra_ref[...]
    d_gate, d_up = (hid_ref[half][:, :hidden] for half in range(2))
    step = 4
    for i in range(n_ctx):
        if i % step == 0:
            for arrival in arrivals[i : i + step]:
                arrival.wait()
        term = (dot(d_gate, w_vmem[i, 0]) + dot(d_up, w_vmem[i, 1])).astype(bf16)
        for k in range(per):
            pair_at, core = divmod(i * per + k, cores)
            sent_ref[core, pair_at * tokens : (pair_at + 1) * tokens] = term[
                :, k * chans : (k + 1) * chans
            ]


def add_kernel(tokens, met_ref, piece_ref, sent_ref):
    cores, _, chans = met_ref.shape
    pairs = sent_ref.shape[0]
    terms = pairs * tokens
    piece = piece_ref[...]
    inner, peak = None, None
    for core in range(cores):
        extra = met_ref[core, terms : terms + EXTRA].astype(f32)[:8]
        part = extra[0:1] + extra[1:2] + extra[2:3]
        top = extra[3:4] + extra[4:5] + extra[5:6]
        inner = part if inner is None else inner + part
        peak = top if peak is None else jnp.maximum(peak, top)
    extra = jnp.concatenate(
        split_rows(inner) + split_rows(peak) + [jnp.zeros((EXTRA - 6, chans), f32)]
    ).astype(bf16)
    for q in range(pairs):
        total = met_ref[0, q * tokens : (q + 1) * tokens].astype(f32)
        for core in range(1, cores):
            total = total + met_ref[core, q * tokens : (q + 1) * tokens].astype(f32)
        sent_ref[q, :tokens] = total.astype(bf16)
        sent_ref[q, tokens : tokens + EXTRA] = extra
        sent_ref[q, tokens + EXTRA :] = piece


def norm_kernel(
    width, back_ref, r_ref, conv_ref, query_ref, gres_ref, gain_ref, inv_ref, dx_ref, dq_ref, sent_ref, mark_ref
):
    peers = back_ref.shape[0]
    chans, tokens = r_ref.shape
    n_ctx = sent_ref.shape[0]
    own = chans // n_ctx
    total = back_ref[0, :tokens].astype(f32)
    extra = back_ref[0, tokens : tokens + EXTRA].astype(f32)[:8]
    inner, peak = extra[0:1] + extra[1:2] + extra[2:3], extra[3:4] + extra[4:5] + extra[5:6]
    for peer in range(1, peers):
        total = total + back_ref[peer, :tokens].astype(f32)
        extra = back_ref[peer, tokens : tokens + EXTRA].astype(f32)[:8]
        inner = inner + (extra[0:1] + extra[1:2] + extra[2:3])
        peak = jnp.maximum(peak, extra[3:4] + extra[4:5] + extra[5:6])
    d_norm = total.T
    resid = r_ref[...]
    inv = inv_ref[...]
    gain = gain_ref[...]
    d_resid = (
        gres_ref[...].astype(f32).T
        + (gain * d_norm) * inv
        - resid * (inv * inv * inner / width)
    )
    dx_ref[...] = d_resid.T.astype(bf16)
    dq_ref[...] = (d_resid * conv_ref[...].astype(f32)).T.astype(bf16)
    d_conv = (d_resid * query_ref[...].astype(f32).T).astype(bf16).astype(f32)
    product = (d_norm * resid * inv).T
    gain_part = jnp.sum(product, axis=0, keepdims=True)
    mark_ref[...] = gain_part
    extra = split_rows(gain_part) + split_rows(peak) + [jnp.zeros((2, chans), f32)]
    for peer in range(n_ctx):
        rows = slice(peer * own, (peer + 1) * own)
        sent_ref[peer] = jnp.concatenate([d_conv[rows]] + extra).astype(bf16)


def rows_kernel(own_ref, other_ref, out_ref):
    peers, _, lanes = own_ref.shape
    blocks = out_ref.shape[0] // lanes
    own = lanes // blocks
    first = lax.axis_index("ch") % 2 == 0
    pieces = []
    for peer in range(peers):
        mine, theirs = own_ref[peer].astype(f32), other_ref[peer].astype(f32)
        pieces += [jnp.where(first, mine, theirs), jnp.where(first, theirs, mine)]
    for a in range(blocks):
        part = jnp.concatenate([piece[a * own : (a + 1) * own] for piece in pieces])
        out_ref[a * lanes : (a + 1) * lanes] = part.T.astype(bf16)


def grad_kernel(back_ref, fre_ref, fim_ref, *refs):
    tables = read_tables(refs[:7])
    ds_ref, gre_ref, gim_ref, dgain_ref, amax_ref = refs[7:]
    n_ctx = back_ref.shape[0]
    own = ds_ref.shape[0] // n_ctx
    blocks = [back_ref[k].astype(f32) for k in range(n_ctx)]
    real, imag = to_spectrum(jnp.concatenate([b[:own] for b in blocks]), tables, True)
    gre_ref[...], gim_ref[...] = real, imag
    fre, fim = fre_ref[...], fim_ref[...]
    back = from_spectrum(real * fre + imag * fim, imag * fre - real * fim, tables)
    ds_ref[...] = back.astype(bf16)
    gain, peak = None, None
    for block in blocks:
        extra = block[own:]
        g = extra[0:1] + extra[1:2] + extra[2:3]
        p = extra[3:4] + extra[4:5] + extra[5:6]
        gain = g if gain is None else gain + g
        peak = p if peak is None else jnp.maximum(peak, p)
    dgain_ref[...] = gain
    amax_ref[...] = jnp.max(peak, axis=1, keepdims=True)


def filter_grad_kernel(gre_ref, gim_ref, sre_ref, sim_ref, *refs):
    tables = read_tables(refs[:7])
    out_ref, mark_ref = refs[7:]
    own = out_ref.shape[0]
    real, imag, sre, sim = gre_ref[...], gim_ref[...], sre_ref[...], sim_ref[...]
    grad = from_spectrum(real * sre + imag * sim, imag * sre - real * sim, tables)
    mark_ref[...] = grad[:1]
    lanes = grad.shape[1]
    for a in range(out_ref.shape[1] // lanes):
        out_ref[:, a * lanes : (a + 1) * lanes] = grad[a * own : (a + 1) * own]


def products_kernel(ds_ref, key_ref, value_ref, dk_ref, dv_ref):
    grad = ds_ref[...].astype(f32).T
    dk_ref[...] = (grad * value_ref[...].astype(f32)).astype(bf16)
    dv_ref[...] = (grad * key_ref[...].astype(f32)).astype(bf16)


def weight_kernel(d_ref, rows_ref, first_ref, second_ref, d_vmem, out_vmem, sems, out_sems):
    n_ctx, _, _, tokens = d_ref.shape
    for copy in load_weights(d_ref, d_vmem, sems):
        copy.wait()
    stores = []
    for half, out_ref in enumerate((first_ref, second_ref)):
        part = jnp.concatenate([d_vmem[i, half] for i in range(n_ctx)], axis=1)
        out_vmem[half] = dot(part, rows_ref[...])
        store = pltpu.make_async_copy(out_vmem.at[half], out_ref, out_sems.at[half])
        store.start()
        stores.append(store)
    for store in stores:
        store.wait()


def on_device(resid_in, query_in, key_in, value_in, filt, gain, w_gate, w_up, g_hid, g_res):
    tokens, chans = resid_in.shape
    n_ctx = lax.axis_size("ctx")
    n_ch = lax.axis_size("ch")
    length = tokens * n_ctx
    rows, hidden = w_gate.shape
    own = chans // n_ctx
    tables = dft_tables(n_ctx, own, tokens)
    spec_rows = tables[6].shape[1]

    def in_hbm(array):
        return pltpu.with_memory_space_constraint(array, pltpu.HBM)

    tables = [in_hbm(jnp.asarray(table)) for table in tables]
    query_near = query_in
    key_in, value_in, resid_in, query_in, filt = (
        in_hbm(array) for array in (key_in, value_in, resid_in, query_in, filt)
    )
    spectrum = ((spec_rows, tokens), f32)
    square = ((chans, tokens), bf16)
    gain_col = gain[:, None]

    mixed, w_both = call(start_kernel, [square, ((2, hidden, rows), bf16)], 4, hbm=(0, 1))(
        key_in, value_in, in_hbm(w_gate.T), in_hbm(w_up.T)
    )
    w_all = in_hbm(lax.all_gather(w_both, "ctx", axis=0, tiled=False))
    spread = lax.all_to_all(mixed.reshape(n_ctx, own, tokens), "ctx", 0, 0, tiled=True)
    kept = [*tables, resid_in, query_in]
    fre, fim, fre_far, fim_far, *kept = call(
        filter_kernel,
        [spectrum] * 4 + [(array.shape, array.dtype) for array in kept],
        len(kept) + 1,
        vmem=(0, 1, *range(4, 4 + len(kept))),
        hbm=(2, 3),
    )(filt, *kept)
    conv, sre, sim = call(conv_kernel, [square, spectrum, spectrum], 10, hbm=(1, 2))(
        spread.reshape(chans, tokens), fre, fim, *kept[:7]
    )
    conv = lax.all_to_all(conv.reshape(n_ctx, own, tokens), "ctx", 0, 0, tiled=True).reshape(
        chans, tokens
    )
    sent, resid = call(
        resid_kernel,
        [((n_ch, chans + EXTRA, tokens), bf16), ((chans, tokens), f32)],
        4,
    )(conv, *kept[7:], gain_col)
    met = lax.all_to_all(sent, "ch", 0, 0, tiled=True)
    share = rows // n_ch
    per = chans // share
    my_ch = lax.axis_index("ch")
    piece = lax.dynamic_slice(
        met.reshape(n_ctx, n_ch // n_ctx, chans + EXTRA, tokens),
        (0, my_ch // per, my_ch % per * share, 0),
        (n_ctx, 1, share, tokens),
    ).reshape(n_ctx, share, tokens)
    piece = lax.all_to_all(piece, "ctx", 0, 0, tiled=True).reshape(n_ctx * share, tokens)
    met, piece = lax.optimization_barrier((met, piece))
    weights = (n_ctx, 2, hidden, rows)
    d_scaled, d_hid, inv, extra = call(
        hidden_kernel,
        [
            ((2, hidden, tokens), bf16),
            ((2, tokens, -(-hidden // 128) * 128), bf16),
            ((1, tokens), f32),
            ((EXTRA, tokens), bf16),
        ],
        5,
        in_specs=[VMEM, HBM, HBM, VMEM, VMEM],
        scratch=[
            pltpu.VMEM(weights, bf16),
            pltpu.VMEM((hidden, tokens), bf16),
            pltpu.SemaphoreType.DMA((n_ctx,)),
            pltpu.SemaphoreType.DMA(()),
        ],
        flops=1e9,
        limit=20,
        hbm=(0,),
    )(met, w_all, in_hbm(g_hid.T), resid, gain_col)
    d_all = in_hbm(lax.all_gather(d_scaled, "ctx", axis=0, tiled=False))
    cores = 2
    pairs = n_ch // cores
    piece_rows = n_ctx * share
    (sent,) = call(
        back_kernel,
        [((cores, pairs * tokens + EXTRA, chans), bf16)],
        3,
        in_specs=[HBM, VMEM, VMEM],
        scratch=[pltpu.VMEM(weights, bf16), pltpu.SemaphoreType.DMA((n_ctx,))],
        flops=1e9,
        limit=20,
    )(w_all, d_hid, extra)
    chip = [[q * cores + core for core in range(cores)] for q in range(pairs)]
    plane = [[q * cores + core for q in range(pairs)] for core in range(cores)]
    met = lax.all_to_all(sent, "ch", 0, 0, tiled=True, axis_index_groups=chip)
    (sent,) = call(
        functools.partial(add_kernel, tokens),
        [((pairs, tokens + EXTRA + piece_rows, chans), bf16)],
        2,
        limit=16,
    )(met, piece)
    back = lax.all_to_all(sent, "ch", 0, 0, tiled=True, axis_index_groups=plane)
    dx, dq, sent, mark = call(
        functools.partial(norm_kernel, chans * n_ch),
        [
            ((tokens, chans), bf16),
            ((tokens, chans), bf16),
            ((n_ctx, 2 * own, tokens), bf16),
            ((1, chans), f32),
        ],
        7,
    )(back, resid, conv, query_near, g_res, gain_col, inv)
    kept = [fre_far, fim_far, *tables]
    kept = call(
        reload_kernel,
        [(array.shape, array.dtype) for array in kept],
        len(kept) + 1,
        vmem=range(len(kept)),
    )(mark, *(in_hbm(array) for array in kept))
    mine = back[:, tokens + EXTRA :]
    back = lax.all_to_all(sent, "ctx", 0, 0, tiled=True)
    ds, gre, gim, dgain, amax = call(
        grad_kernel,
        [square, spectrum, spectrum, ((1, chans), f32), ((1, 1), f32)],
        10,
        hbm=(1, 2),
    )(back, *kept)
    ds = lax.all_to_all(ds.reshape(n_ctx, own, tokens), "ctx", 0, 0, tiled=True)
    dfilt, mark = call(filter_grad_kernel, [(filt.shape, f32), ((1, tokens), f32)], 11)(
        *(in_hbm(array) for array in (gre, gim, sre, sim)), *tables
    )
    mine, mark = lax.optimization_barrier((mine, mark))
    theirs = lax.ppermute(mine, "ch", [(j, j + 1 - 2 * (j % 2)) for j in range(n_ch)])
    (row_acts,) = call(rows_kernel, [((length, rows), bf16)], 2)(mine, theirs)
    dk, dv = call(products_kernel, [((tokens, chans), bf16)] * 2, 3)(
        ds.reshape(chans, tokens), key_in, value_in
    )
    first, second = call(
        weight_kernel,
        [((hidden, rows), f32)] * 2,
        2,
        in_specs=[HBM, VMEM],
        out_specs=[HBM, HBM],
        scratch=[
            pltpu.VMEM((n_ctx, 2, hidden, tokens), bf16),
            pltpu.VMEM((2, hidden, rows), f32),
            pltpu.SemaphoreType.DMA((n_ctx,)),
            pltpu.SemaphoreType.DMA((2,)),
        ],
        hbm=(0, 1),
        flops=1e9,
        limit=16,
    )(d_all, row_acts)
    return (dx, dq, dk, dv, dfilt, dgain[0], first.T, second.T, amax[0, 0])


def solution(mesh):
    return jax.shard_map(
        on_device,
        mesh=mesh,
        in_specs=(
            P("ctx", "ch"),
            P("ctx", "ch"),
            P("ctx", "ch"),
            P("ctx", "ch"),
            P(("ch", "ctx"), None),
            P("ch"),
            P("ctx", "ch"),
            P("ctx", "ch"),
            P("ctx", "ch"),
            P("ctx", "ch"),
        ),
        out_specs=(
            P("ctx", "ch"),
            P("ctx", "ch"),
            P("ctx", "ch"),
            P("ctx", "ch"),
            P(("ch", "ctx"), None),
            P("ch"),
            P("ctx", "ch"),
            P("ctx", "ch"),
            P(),
        ),
        check_vma=False,
    )
```

```python
import functools
import math

import jax
import jax.numpy as jnp
import numpy as np
from jax import lax
from jax.experimental import pallas as pl
from jax.experimental.pallas import tpu as pltpu
from jax.sharding import PartitionSpec as P

epsilon = 1e-06
f32 = jnp.float32
bf16 = jnp.bfloat16
VMEM = pl.BlockSpec(memory_space=pltpu.VMEM)
HBM = pl.BlockSpec(memory_space=pltpu.HBM)
EXTRA = 16


def call(body, outs, n_in, flops=1e3, in_specs=None, out_specs=None, scratch=(), limit=8, hbm=(), vmem=()):
    return pl.pallas_call(
        body,
        out_shape=tuple(
            pltpu.HBM(s, d) if k in hbm else pltpu.VMEM(s, d) if k in vmem else jax.ShapeDtypeStruct(s, d)
            for k, (s, d) in enumerate(outs)
        ),
        in_specs=in_specs or [VMEM] * n_in,
        out_specs=tuple(out_specs or [VMEM] * len(outs)),
        scratch_shapes=list(scratch),
        compiler_params=pltpu.CompilerParams(vmem_limit_bytes=limit * 2**20),
        cost_estimate=pl.CostEstimate(flops=int(flops), bytes_accessed=int(flops / 1e3), transcendentals=0),
    )


def split_table(table):
    high = table.astype(np.float32).astype(jnp.bfloat16)
    low = (table - high.astype(np.float64)).astype(np.float32).astype(jnp.bfloat16)
    return np.asarray(high), np.asarray(low)


@functools.cache
def dft_tables(blocks, chans, lanes):
    turns = 2 * blocks
    half = blocks + 1
    total = turns * lanes
    freq = np.arange(half)
    eye = np.eye(chans)
    angle = 2.0 * np.pi * (np.outer(freq, np.arange(blocks)) % turns) / turns
    first = np.concatenate([np.kron(np.cos(angle), eye), np.kron(-np.sin(angle), eye)])
    weight = np.where((freq == 0) | (freq == blocks), 1.0, 2.0)[:, None] / total
    last = np.concatenate(
        [np.kron(weight * np.cos(angle), eye), np.kron(-weight * np.sin(angle), eye)]
    ).T
    angle = 2.0 * np.pi * (np.outer(np.arange(lanes), np.arange(lanes)) % lanes) / lanes
    inner = np.concatenate([np.cos(angle), np.sin(angle)], axis=1)
    angle = 2.0 * np.pi * np.repeat(np.outer(freq, np.arange(lanes)), chans, axis=0) / total
    twiddle = np.stack([np.cos(angle), np.sin(angle)]).astype(np.float32)
    last = np.pad(last, ((0, 0), (0, -last.shape[1] % lanes)))
    wide = [np.concatenate(np.split(t, t.shape[1] // lanes, axis=1)) for t in (last, inner)]
    return (*split_table(first), *split_table(wide[0]), *split_table(wide[1]), twiddle)


def read_tables(refs):
    tables = []
    for ref in refs:
        table = ref[...]
        if 2 <= len(tables) < 6:
            lanes = table.shape[1]
            table = jnp.concatenate(
                [table[k : k + lanes] for k in range(0, table.shape[0], lanes)], axis=1
            )
        tables.append(table)
    return tables


def pair(value):
    high = value.astype(bf16)
    return high, (value - high.astype(f32)).astype(bf16)


def dot(left, right):
    return jnp.dot(left, right, preferred_element_type=f32)


def turn_lanes(parts, inner_hi, inner_lo, lanes, sign):
    rows = parts.shape[0] // 2
    high, low = pair(parts)
    both = dot(high, inner_hi) + (dot(high, inner_lo) + dot(low, inner_hi))
    by_cos, by_sin = both[:, :lanes], both[:, lanes:]
    real = by_cos[:rows] - sign * by_sin[rows:]
    imag = by_cos[rows:] + sign * by_sin[:rows]
    return real, imag


def to_spectrum(signal, tables, exact):
    first_hi, first_lo, _, _, inner_hi, inner_lo, twiddle = tables
    lanes = signal.shape[1]
    if exact:
        signal = signal.astype(bf16)
        out = dot(first_hi, signal) + dot(first_lo, signal)
    else:
        high, low = pair(signal)
        out = dot(first_hi, high) + (dot(first_hi, low) + dot(first_lo, high))
    rows = out.shape[0] // 2
    real, imag = out[:rows], out[rows:]
    cos, sin = twiddle[0], twiddle[1]
    turned = jnp.concatenate([real * cos + imag * sin, imag * cos - real * sin])
    return turn_lanes(turned, inner_hi, inner_lo, lanes, -1.0)


def from_spectrum(real, imag, tables):
    _, _, last_hi, last_lo, inner_hi, inner_lo, twiddle = tables
    lanes = real.shape[1]
    real, imag = turn_lanes(jnp.concatenate([real, imag]), inner_hi, inner_lo, lanes, 1.0)
    cos, sin = twiddle[0], twiddle[1]
    both = jnp.concatenate([real * cos - imag * sin, real * sin + imag * cos])
    rest = jnp.zeros((last_hi.shape[1] - both.shape[0], lanes), f32)
    high, low = pair(jnp.concatenate([both, rest]))
    return dot(last_hi, high) + (dot(last_hi, low) + dot(last_lo, high))


def split_rows(row):
    high = row.astype(bf16).astype(f32)
    rest = row - high
    mid = rest.astype(bf16).astype(f32)
    low = rest - mid
    return [high, mid, low]


def start_kernel(key_ref, value_ref, gate_ref, up_ref, mixed_ref, w_ref):
    w_ref[0] = gate_ref[...]
    w_ref[1] = up_ref[...]
    mixed = (key_ref[...].astype(f32) * value_ref[...].astype(f32)).astype(bf16)
    mixed_ref[...] = mixed.astype(f32).T.astype(bf16)


def reload_kernel(mark_ref, *refs):
    half = len(refs) // 2
    for source, copy in zip(refs[:half], refs[half:]):
        copy[...] = source[...]


def filter_kernel(filt_ref, *refs):
    n_kept = (len(refs) - 4) // 2
    kept, spectra, copies = refs[:n_kept], refs[n_kept : n_kept + 4], refs[n_kept + 4 :]
    for source, copy in zip(kept, copies):
        copy[...] = source[...]
    tables = read_tables(kept[:7])
    lanes = kept[0].shape[1]
    blocks = filt_ref.shape[1] // lanes
    signal = jnp.concatenate([filt_ref[:, a * lanes : (a + 1) * lanes] for a in range(blocks)])
    real, imag = to_spectrum(signal, tables, False)
    for k in range(2):
        spectra[2 * k][...], spectra[2 * k + 1][...] = real, imag


def conv_kernel(src_ref, fre_ref, fim_ref, *refs):
    tables = read_tables(refs[:7])
    conv_ref, sre_ref, sim_ref = refs[7:]
    real, imag = to_spectrum(src_ref[...], tables, True)
    sre_ref[...], sim_ref[...] = real, imag
    fre, fim = fre_ref[...], fim_ref[...]
    conv = from_spectrum(real * fre - imag * fim, real * fim + imag * fre, tables)
    conv_ref[...] = conv.astype(bf16)


def resid_kernel(conv_ref, resid_ref, query_ref, gain_ref, sent_ref, r_ref):
    chans, tokens = conv_ref.shape
    resid = resid_ref[...].astype(f32).T + query_ref[...].astype(f32).T * conv_ref[...].astype(f32)
    r_ref[...] = resid
    scaled = (resid * gain_ref[...]).astype(bf16)
    square = jnp.sum(resid * resid, axis=0, keepdims=True)
    extra = jnp.concatenate(split_rows(square) + [jnp.zeros((EXTRA - 3, tokens), f32)]).astype(bf16)
    for peer in range(sent_ref.shape[0]):
        sent_ref[peer, :chans] = scaled
        sent_ref[peer, chans:] = extra


def load_weights(w_ref, w_vmem, sems):
    copies = [
        pltpu.make_async_copy(w_ref.at[i], w_vmem.at[i], sems.at[i]) for i in range(w_ref.shape[0])
    ]
    for copy in copies:
        copy.start()
    return copies


def hidden_kernel(
    met_ref, w_ref, grad_ref, r_ref, gain_ref, d_ref, hid_ref, inv_ref, extra_ref, w_vmem, grad_vmem, sems, grad_sem
):
    copies = load_weights(w_ref, w_vmem, sems)
    grad_copy = pltpu.make_async_copy(grad_ref, grad_vmem, grad_sem)
    grad_copy.start()
    n_ch, _, tokens = met_ref.shape
    chans = r_ref.shape[0]
    per = w_ref.shape[3] // chans
    total = jnp.zeros((8, tokens), f32)
    for peer in range(n_ch):
        total = total + met_ref[peer, chans : chans + EXTRA].astype(f32)[:8]
    inv = lax.rsqrt((total[0:1] + total[1:2] + total[2:3]) / (n_ch * chans) + epsilon)
    inv_ref[...] = inv
    amax = jnp.max(jnp.abs((r_ref[...] * gain_ref[...]) * inv), axis=0, keepdims=True)
    amax = jnp.max(amax, axis=1, keepdims=True)
    gate, up = None, None
    for i, copy in enumerate(copies):
        copy.wait()
        acts = jnp.concatenate([met_ref[i * per + k, :chans] for k in range(per)])
        part = dot(w_vmem[i, 0], acts)
        gate = part if gate is None else gate + part
        part = dot(w_vmem[i, 1], acts)
        up = part if up is None else up + part
    gate, up = gate * inv, up * inv
    sigma = 1.0 / (1.0 + jnp.exp(-gate))
    grad_copy.wait()
    hid = grad_vmem[...].astype(f32)
    d_gate = hid * up * sigma * (1.0 + gate * (1.0 - sigma))
    d_up = hid * gate * sigma
    d_ref[0] = (d_gate * inv).astype(bf16)
    d_ref[1] = (d_up * inv).astype(bf16)
    hid_ref[0] = d_gate.astype(bf16)
    hid_ref[1] = d_up.astype(bf16)
    inner = jnp.sum(d_gate * gate + d_up * up, axis=0, keepdims=True)
    extra_ref[...] = jnp.concatenate(
        split_rows(inner)
        + split_rows(jnp.broadcast_to(amax, (1, tokens)))
        + [jnp.zeros((EXTRA - 6, tokens), f32)]
    ).astype(bf16)


def back_kernel(w_ref, hid_ref, extra_ref, sent_ref, w_vmem, sems):
    arrivals = load_weights(w_ref, w_vmem, sems)
    tokens = hid_ref.shape[2]
    cores, _, chans = sent_ref.shape
    n_ctx, _, hidden, rows = w_ref.shape
    per = rows // chans
    terms = n_ctx * per // cores * tokens
    for core in range(cores):
        sent_ref[core, terms:] = extra_ref[...]
    rest = jnp.zeros((-hidden % 128, tokens), f32)
    d_gate, d_up = (
        jnp.concatenate([hid_ref[half].astype(f32), rest]).T.astype(bf16)[:, :hidden]
        for half in range(2)
    )
    step = 4
    for i in range(n_ctx):
        if i % step == 0:
            for arrival in arrivals[i : i + step]:
                arrival.wait()
        term = (dot(d_gate, w_vmem[i, 0]) + dot(d_up, w_vmem[i, 1])).astype(bf16)
        for k in range(per):
            pair_at, core = divmod(i * per + k, cores)
            sent_ref[core, pair_at * tokens : (pair_at + 1) * tokens] = term[
                :, k * chans : (k + 1) * chans
            ]


def add_kernel(tokens, met_ref, piece_ref, sent_ref):
    cores, _, chans = met_ref.shape
    pairs = sent_ref.shape[0]
    terms = pairs * tokens
    piece = piece_ref[...]
    inner, peak = None, None
    for core in range(cores):
        extra = met_ref[core, terms : terms + EXTRA].astype(f32)[:8]
        part = extra[0:1] + extra[1:2] + extra[2:3]
        top = extra[3:4] + extra[4:5] + extra[5:6]
        inner = part if inner is None else inner + part
        peak = top if peak is None else jnp.maximum(peak, top)
    extra = jnp.concatenate(
        split_rows(inner) + split_rows(peak) + [jnp.zeros((EXTRA - 6, chans), f32)]
    ).astype(bf16)
    for q in range(pairs):
        total = met_ref[0, q * tokens : (q + 1) * tokens].astype(f32)
        for core in range(1, cores):
            total = total + met_ref[core, q * tokens : (q + 1) * tokens].astype(f32)
        sent_ref[q, :tokens] = total.astype(bf16)
        sent_ref[q, tokens : tokens + EXTRA] = extra
        sent_ref[q, tokens + EXTRA :] = piece


def norm_kernel(
    width, back_ref, r_ref, conv_ref, query_ref, gres_ref, gain_ref, inv_ref, dx_ref, dq_ref, sent_ref, mark_ref
):
    peers = back_ref.shape[0]
    chans, tokens = r_ref.shape
    n_ctx = sent_ref.shape[0]
    own = chans // n_ctx
    total = back_ref[0, :tokens].astype(f32)
    extra = back_ref[0, tokens : tokens + EXTRA].astype(f32)[:8]
    inner, peak = extra[0:1] + extra[1:2] + extra[2:3], extra[3:4] + extra[4:5] + extra[5:6]
    for peer in range(1, peers):
        total = total + back_ref[peer, :tokens].astype(f32)
        extra = back_ref[peer, tokens : tokens + EXTRA].astype(f32)[:8]
        inner = inner + (extra[0:1] + extra[1:2] + extra[2:3])
        peak = jnp.maximum(peak, extra[3:4] + extra[4:5] + extra[5:6])
    d_norm = total.T
    resid = r_ref[...]
    inv = inv_ref[...]
    gain = gain_ref[...]
    d_resid = (
        gres_ref[...].astype(f32).T
        + (gain * d_norm) * inv
        - resid * (inv * inv * inner / width)
    )
    dx_ref[...] = d_resid.T.astype(bf16)
    dq_ref[...] = (d_resid * conv_ref[...].astype(f32)).T.astype(bf16)
    d_conv = (d_resid * query_ref[...].astype(f32).T).astype(bf16).astype(f32)
    product = (d_norm * resid * inv).T
    gain_part = jnp.sum(product, axis=0, keepdims=True)
    mark_ref[...] = gain_part
    extra = split_rows(gain_part) + split_rows(peak) + [jnp.zeros((2, chans), f32)]
    for peer in range(n_ctx):
        rows = slice(peer * own, (peer + 1) * own)
        sent_ref[peer] = jnp.concatenate([d_conv[rows]] + extra).astype(bf16)


def rows_kernel(own_ref, other_ref, out_ref):
    peers, _, lanes = own_ref.shape
    blocks = out_ref.shape[0] // lanes
    own = lanes // blocks
    first = lax.axis_index("ch") % 2 == 0
    pieces = []
    for peer in range(peers):
        mine, theirs = own_ref[peer].astype(f32), other_ref[peer].astype(f32)
        pieces += [jnp.where(first, mine, theirs), jnp.where(first, theirs, mine)]
    for a in range(blocks):
        part = jnp.concatenate([piece[a * own : (a + 1) * own] for piece in pieces])
        out_ref[a * lanes : (a + 1) * lanes] = part.T.astype(bf16)


def grad_kernel(back_ref, fre_ref, fim_ref, *refs):
    tables = read_tables(refs[:7])
    ds_ref, gre_ref, gim_ref, dgain_ref, amax_ref = refs[7:]
    n_ctx = back_ref.shape[0]
    own = ds_ref.shape[0] // n_ctx
    blocks = [back_ref[k].astype(f32) for k in range(n_ctx)]
    real, imag = to_spectrum(jnp.concatenate([b[:own] for b in blocks]), tables, True)
    gre_ref[...], gim_ref[...] = real, imag
    fre, fim = fre_ref[...], fim_ref[...]
    back = from_spectrum(real * fre + imag * fim, imag * fre - real * fim, tables)
    ds_ref[...] = back.astype(bf16)
    gain, peak = None, None
    for block in blocks:
        extra = block[own:]
        g = extra[0:1] + extra[1:2] + extra[2:3]
        p = extra[3:4] + extra[4:5] + extra[5:6]
        gain = g if gain is None else gain + g
        peak = p if peak is None else jnp.maximum(peak, p)
    dgain_ref[...] = gain
    amax_ref[...] = jnp.max(peak, axis=1, keepdims=True)


def filter_grad_kernel(gre_ref, gim_ref, sre_ref, sim_ref, *refs):
    tables = read_tables(refs[:7])
    out_ref = refs[7]
    own = out_ref.shape[0]
    real, imag, sre, sim = gre_ref[...], gim_ref[...], sre_ref[...], sim_ref[...]
    grad = from_spectrum(real * sre + imag * sim, imag * sre - real * sim, tables)
    lanes = grad.shape[1]
    for a in range(out_ref.shape[1] // lanes):
        out_ref[:, a * lanes : (a + 1) * lanes] = grad[a * own : (a + 1) * own]


def products_kernel(ds_ref, key_ref, value_ref, dk_ref, dv_ref):
    grad = ds_ref[...].astype(f32).T
    dk_ref[...] = (grad * value_ref[...].astype(f32)).astype(bf16)
    dv_ref[...] = (grad * key_ref[...].astype(f32)).astype(bf16)


def weight_kernel(d_ref, rows_ref, first_ref, second_ref, d_vmem, out_vmem, sems, out_sems):
    n_ctx, _, _, tokens = d_ref.shape
    for copy in load_weights(d_ref, d_vmem, sems):
        copy.wait()
    stores = []
    for half, out_ref in enumerate((first_ref, second_ref)):
        part = jnp.concatenate([d_vmem[i, half] for i in range(n_ctx)], axis=1)
        out_vmem[half] = dot(part, rows_ref[...])
        store = pltpu.make_async_copy(out_vmem.at[half], out_ref, out_sems.at[half])
        store.start()
        stores.append(store)
    for store in stores:
        store.wait()


def on_device(resid_in, query_in, key_in, value_in, filt, gain, w_gate, w_up, g_hid, g_res):
    tokens, chans = resid_in.shape
    n_ctx = lax.axis_size("ctx")
    n_ch = lax.axis_size("ch")
    length = tokens * n_ctx
    rows, hidden = w_gate.shape
    own = chans // n_ctx
    tables = dft_tables(n_ctx, own, tokens)
    spec_rows = tables[6].shape[1]

    def in_hbm(array):
        return pltpu.with_memory_space_constraint(array, pltpu.HBM)

    tables = [in_hbm(jnp.asarray(table)) for table in tables]
    query_near = query_in
    key_in, value_in, resid_in, query_in, filt = (
        in_hbm(array) for array in (key_in, value_in, resid_in, query_in, filt)
    )
    spectrum = ((spec_rows, tokens), f32)
    square = ((chans, tokens), bf16)
    gain_col = gain[:, None]

    mixed, w_both = call(start_kernel, [square, ((2, hidden, rows), bf16)], 4, hbm=(0, 1))(
        key_in, value_in, in_hbm(w_gate.T), in_hbm(w_up.T)
    )
    w_all = in_hbm(lax.all_gather(w_both, "ctx", axis=0, tiled=False))
    spread = lax.all_to_all(mixed.reshape(n_ctx, own, tokens), "ctx", 0, 0, tiled=True)
    kept = [*tables, resid_in, query_in]
    fre, fim, fre_far, fim_far, *kept = call(
        filter_kernel,
        [spectrum] * 4 + [(array.shape, array.dtype) for array in kept],
        len(kept) + 1,
        vmem=(0, 1, *range(4, 4 + len(kept))),
        hbm=(2, 3),
    )(filt, *kept)
    conv, sre, sim = call(conv_kernel, [square, spectrum, spectrum], 10, hbm=(1, 2))(
        spread.reshape(chans, tokens), fre, fim, *kept[:7]
    )
    conv = lax.all_to_all(conv.reshape(n_ctx, own, tokens), "ctx", 0, 0, tiled=True).reshape(
        chans, tokens
    )
    sent, resid = call(
        resid_kernel,
        [((n_ch, chans + EXTRA, tokens), bf16), ((chans, tokens), f32)],
        4,
    )(conv, *kept[7:], gain_col)
    met = lax.all_to_all(sent, "ch", 0, 0, tiled=True)
    share = rows // n_ch
    per = chans // share
    my_ch = lax.axis_index("ch")
    piece = lax.dynamic_slice(
        met.reshape(n_ctx, n_ch // n_ctx, chans + EXTRA, tokens),
        (0, my_ch // per, my_ch % per * share, 0),
        (n_ctx, 1, share, tokens),
    ).reshape(n_ctx, share, tokens)
    piece = lax.all_to_all(piece, "ctx", 0, 0, tiled=True).reshape(n_ctx * share, tokens)
    met, piece = lax.optimization_barrier((met, piece))
    weights = (n_ctx, 2, hidden, rows)
    d_scaled, d_hid, inv, extra = call(
        hidden_kernel,
        [
            ((2, hidden, tokens), bf16),
            ((2, hidden, tokens), bf16),
            ((1, tokens), f32),
            ((EXTRA, tokens), bf16),
        ],
        5,
        in_specs=[VMEM, HBM, HBM, VMEM, VMEM],
        scratch=[
            pltpu.VMEM(weights, bf16),
            pltpu.VMEM((hidden, tokens), bf16),
            pltpu.SemaphoreType.DMA((n_ctx,)),
            pltpu.SemaphoreType.DMA(()),
        ],
        flops=1e9,
        limit=20,
        hbm=(0,),
    )(met, w_all, in_hbm(g_hid.T), resid, gain_col)
    d_all = in_hbm(lax.all_gather(d_scaled, "ctx", axis=0, tiled=False))
    cores = 2
    pairs = n_ch // cores
    piece_rows = n_ctx * share
    (sent,) = call(
        back_kernel,
        [((cores, pairs * tokens + EXTRA, chans), bf16)],
        3,
        in_specs=[HBM, VMEM, VMEM],
        scratch=[pltpu.VMEM(weights, bf16), pltpu.SemaphoreType.DMA((n_ctx,))],
        flops=1e9,
        limit=20,
    )(w_all, d_hid, extra)
    chip = [[q * cores + core for core in range(cores)] for q in range(pairs)]
    plane = [[q * cores + core for q in range(pairs)] for core in range(cores)]
    met = lax.all_to_all(sent, "ch", 0, 0, tiled=True, axis_index_groups=chip)
    (sent,) = call(
        functools.partial(add_kernel, tokens),
        [((pairs, tokens + EXTRA + piece_rows, chans), bf16)],
        2,
        limit=16,
    )(met, piece)
    back = lax.all_to_all(sent, "ch", 0, 0, tiled=True, axis_index_groups=plane)
    dx, dq, sent, mark = call(
        functools.partial(norm_kernel, chans * n_ch),
        [
            ((tokens, chans), bf16),
            ((tokens, chans), bf16),
            ((n_ctx, 2 * own, tokens), bf16),
            ((1, chans), f32),
        ],
        7,
    )(back, resid, conv, query_near, g_res, gain_col, inv)

    def reload(mark, arrays):
        return list(
            call(
                reload_kernel,
                [(array.shape, array.dtype) for array in arrays],
                len(arrays) + 1,
                vmem=range(len(arrays)),
            )(mark, *(in_hbm(array) for array in arrays))
        )

    mine, mark = lax.optimization_barrier((back[:, tokens + EXTRA :], mark))
    kept = reload(mark, [fre_far, fim_far, *tables])
    theirs = lax.ppermute(mine, "ch", [(j, j + 1 - 2 * (j % 2)) for j in range(n_ch)])
    (row_acts,) = call(rows_kernel, [((length, rows), bf16)], 2)(mine, theirs)
    kept[0], row_acts = lax.optimization_barrier((kept[0], row_acts))
    back = lax.all_to_all(sent, "ctx", 0, 0, tiled=True)
    ds, gre, gim, dgain, amax = call(
        grad_kernel,
        [square, spectrum, spectrum, ((1, chans), f32), ((1, 1), f32)],
        10,
        hbm=(1, 2),
    )(back, *kept)
    ds = lax.all_to_all(ds.reshape(n_ctx, own, tokens), "ctx", 0, 0, tiled=True)
    (dfilt,) = call(filter_grad_kernel, [(filt.shape, f32)], 11)(
        *(in_hbm(array) for array in (gre, gim, sre, sim)), *tables
    )
    key_near, value_near = reload(dgain, [key_in, value_in])
    dk, dv = call(products_kernel, [((tokens, chans), bf16)] * 2, 3)(
        ds.reshape(chans, tokens), key_near, value_near
    )
    first, second = call(
        weight_kernel,
        [((hidden, rows), f32)] * 2,
        2,
        in_specs=[HBM, VMEM],
        out_specs=[HBM, HBM],
        scratch=[
            pltpu.VMEM((n_ctx, 2, hidden, tokens), bf16),
            pltpu.VMEM((2, hidden, rows), f32),
            pltpu.SemaphoreType.DMA((n_ctx,)),
            pltpu.SemaphoreType.DMA((2,)),
        ],
        hbm=(0, 1),
        flops=1e9,
        limit=16,
    )(d_all, row_acts)
    return (dx, dq, dk, dv, dfilt, dgain[0], first.T, second.T, amax[0, 0])


def solution(mesh):
    return jax.shard_map(
        on_device,
        mesh=mesh,
        in_specs=(
            P("ctx", "ch"),
            P("ctx", "ch"),
            P("ctx", "ch"),
            P("ctx", "ch"),
            P(("ch", "ctx"), None),
            P("ch"),
            P("ctx", "ch"),
            P("ctx", "ch"),
            P("ctx", "ch"),
            P("ctx", "ch"),
        ),
        out_specs=(
            P("ctx", "ch"),
            P("ctx", "ch"),
            P("ctx", "ch"),
            P("ctx", "ch"),
            P(("ch", "ctx"), None),
            P("ch"),
            P("ctx", "ch"),
            P("ctx", "ch"),
            P(),
        ),
        check_vma=False,
    )
```

```python
import functools
import math

import jax
import jax.numpy as jnp
import numpy as np
from jax import lax
from jax.experimental import pallas as pl
from jax.experimental.pallas import tpu as pltpu
from jax.sharding import PartitionSpec as P

epsilon = 1e-06
f32 = jnp.float32
bf16 = jnp.bfloat16
VMEM = pl.BlockSpec(memory_space=pltpu.VMEM)
HBM = pl.BlockSpec(memory_space=pltpu.HBM)
EXTRA = 16


def call(body, outs, n_in, flops=1e3, in_specs=None, out_specs=None, scratch=(), limit=8, hbm=(), vmem=()):
    return pl.pallas_call(
        body,
        out_shape=tuple(
            pltpu.HBM(s, d) if k in hbm else pltpu.VMEM(s, d) if k in vmem else jax.ShapeDtypeStruct(s, d)
            for k, (s, d) in enumerate(outs)
        ),
        in_specs=in_specs or [VMEM] * n_in,
        out_specs=tuple(out_specs or [VMEM] * len(outs)),
        scratch_shapes=list(scratch),
        compiler_params=pltpu.CompilerParams(vmem_limit_bytes=limit * 2**20),
        cost_estimate=pl.CostEstimate(flops=int(flops), bytes_accessed=int(flops / 1e3), transcendentals=0),
    )


def split_table(table):
    high = table.astype(np.float32).astype(jnp.bfloat16)
    low = (table - high.astype(np.float64)).astype(np.float32).astype(jnp.bfloat16)
    return np.asarray(high), np.asarray(low)


@functools.cache
def dft_tables(blocks, chans, lanes):
    turns = 2 * blocks
    half = blocks + 1
    total = turns * lanes
    freq = np.arange(half)
    eye = np.eye(chans)
    angle = 2.0 * np.pi * (np.outer(freq, np.arange(blocks)) % turns) / turns
    first = np.concatenate([np.kron(np.cos(angle), eye), np.kron(-np.sin(angle), eye)])
    weight = np.where((freq == 0) | (freq == blocks), 1.0, 2.0)[:, None] / total
    last = np.concatenate(
        [np.kron(weight * np.cos(angle), eye), np.kron(-weight * np.sin(angle), eye)]
    ).T
    angle = 2.0 * np.pi * (np.outer(np.arange(lanes), np.arange(lanes)) % lanes) / lanes
    inner = np.concatenate([np.cos(angle), np.sin(angle)], axis=1)
    angle = 2.0 * np.pi * np.repeat(np.outer(freq, np.arange(lanes)), chans, axis=0) / total
    twiddle = np.stack([np.cos(angle), np.sin(angle)]).astype(np.float32)
    last = np.pad(last, ((0, 0), (0, -last.shape[1] % lanes)))
    wide = [np.concatenate(np.split(t, t.shape[1] // lanes, axis=1)) for t in (last, inner)]
    return (*split_table(first), *split_table(wide[0]), *split_table(wide[1]), twiddle)


def read_tables(refs):
    tables = []
    for ref in refs:
        table = ref[...]
        if 2 <= len(tables) < 6:
            lanes = table.shape[1]
            table = jnp.concatenate(
                [table[k : k + lanes] for k in range(0, table.shape[0], lanes)], axis=1
            )
        tables.append(table)
    return tables


def pair(value):
    high = value.astype(bf16)
    return high, (value - high.astype(f32)).astype(bf16)


def dot(left, right):
    return jnp.dot(left, right, preferred_element_type=f32)


def turn_lanes(parts, inner_hi, inner_lo, lanes, sign):
    rows = parts.shape[0] // 2
    high, low = pair(parts)
    both = dot(high, inner_hi) + (dot(high, inner_lo) + dot(low, inner_hi))
    by_cos, by_sin = both[:, :lanes], both[:, lanes:]
    real = by_cos[:rows] - sign * by_sin[rows:]
    imag = by_cos[rows:] + sign * by_sin[:rows]
    return real, imag


def to_spectrum(signal, tables, exact):
    first_hi, first_lo, _, _, inner_hi, inner_lo, twiddle = tables
    lanes = signal.shape[1]
    if exact:
        signal = signal.astype(bf16)
        out = dot(first_hi, signal) + dot(first_lo, signal)
    else:
        high, low = pair(signal)
        out = dot(first_hi, high) + (dot(first_hi, low) + dot(first_lo, high))
    rows = out.shape[0] // 2
    real, imag = out[:rows], out[rows:]
    cos, sin = twiddle[0], twiddle[1]
    turned = jnp.concatenate([real * cos + imag * sin, imag * cos - real * sin])
    return turn_lanes(turned, inner_hi, inner_lo, lanes, -1.0)


def from_spectrum(real, imag, tables):
    _, _, last_hi, last_lo, inner_hi, inner_lo, twiddle = tables
    lanes = real.shape[1]
    real, imag = turn_lanes(jnp.concatenate([real, imag]), inner_hi, inner_lo, lanes, 1.0)
    cos, sin = twiddle[0], twiddle[1]
    both = jnp.concatenate([real * cos - imag * sin, real * sin + imag * cos])
    rest = jnp.zeros((last_hi.shape[1] - both.shape[0], lanes), f32)
    high, low = pair(jnp.concatenate([both, rest]))
    return dot(last_hi, high) + (dot(last_hi, low) + dot(last_lo, high))


def split_rows(row):
    high = row.astype(bf16).astype(f32)
    rest = row - high
    mid = rest.astype(bf16).astype(f32)
    low = rest - mid
    return [high, mid, low]


def start_kernel(key_ref, value_ref, gate_ref, up_ref, mixed_ref, w_ref):
    w_ref[0] = gate_ref[...]
    w_ref[1] = up_ref[...]
    mixed = (key_ref[...].astype(f32) * value_ref[...].astype(f32)).astype(bf16)
    mixed_ref[...] = mixed.astype(f32).T.astype(bf16)


def reload_kernel(mark_ref, *refs):
    half = len(refs) // 2
    for source, copy in zip(refs[:half], refs[half:]):
        copy[...] = source[...]


def filter_kernel(filt_ref, *refs):
    n_kept = (len(refs) - 4) // 2
    kept, spectra, copies = refs[:n_kept], refs[n_kept : n_kept + 4], refs[n_kept + 4 :]
    for source, copy in zip(kept, copies):
        copy[...] = source[...]
    tables = read_tables(kept[:7])
    lanes = kept[0].shape[1]
    blocks = filt_ref.shape[1] // lanes
    signal = jnp.concatenate([filt_ref[:, a * lanes : (a + 1) * lanes] for a in range(blocks)])
    real, imag = to_spectrum(signal, tables, False)
    for k in range(2):
        spectra[2 * k][...], spectra[2 * k + 1][...] = real, imag


def conv_kernel(src_ref, fre_ref, fim_ref, *refs):
    tables = read_tables(refs[:7])
    conv_ref, sre_ref, sim_ref = refs[7:]
    real, imag = to_spectrum(src_ref[...], tables, True)
    sre_ref[...], sim_ref[...] = real, imag
    fre, fim = fre_ref[...], fim_ref[...]
    conv = from_spectrum(real * fre - imag * fim, real * fim + imag * fre, tables)
    conv_ref[...] = conv.astype(bf16)


def resid_kernel(conv_ref, resid_ref, query_ref, gain_ref, sent_ref, r_ref):
    chans, tokens = conv_ref.shape
    resid = resid_ref[...].astype(f32).T + query_ref[...].astype(f32).T * conv_ref[...].astype(f32)
    r_ref[...] = resid
    scaled = (resid * gain_ref[...]).astype(bf16)
    square = jnp.sum(resid * resid, axis=0, keepdims=True)
    extra = jnp.concatenate(split_rows(square) + [jnp.zeros((EXTRA - 3, tokens), f32)]).astype(bf16)
    for peer in range(sent_ref.shape[0]):
        sent_ref[peer, :chans] = scaled
        sent_ref[peer, chans:] = extra


def load_weights(w_ref, w_vmem, sems):
    copies = [
        pltpu.make_async_copy(w_ref.at[i], w_vmem.at[i], sems.at[i]) for i in range(w_ref.shape[0])
    ]
    for copy in copies:
        copy.start()
    return copies


def hidden_kernel(
    met_ref, w_ref, grad_ref, r_ref, gain_ref, d_ref, hid_ref, inv_ref, extra_ref, w_vmem, grad_vmem, sems, grad_sem
):
    copies = load_weights(w_ref, w_vmem, sems)
    grad_copy = pltpu.make_async_copy(grad_ref, grad_vmem, grad_sem)
    grad_copy.start()
    n_ch, _, tokens = met_ref.shape
    chans = r_ref.shape[0]
    per = w_ref.shape[3] // chans
    total = jnp.zeros((8, tokens), f32)
    for peer in range(n_ch):
        total = total + met_ref[peer, chans : chans + EXTRA].astype(f32)[:8]
    inv = lax.rsqrt((total[0:1] + total[1:2] + total[2:3]) / (n_ch * chans) + epsilon)
    inv_ref[...] = inv
    amax = jnp.max(jnp.abs((r_ref[...] * gain_ref[...]) * inv), axis=0, keepdims=True)
    amax = jnp.max(amax, axis=1, keepdims=True)
    gate, up = None, None
    for i, copy in enumerate(copies):
        copy.wait()
        acts = jnp.concatenate([met_ref[i * per + k, :chans] for k in range(per)])
        part = dot(w_vmem[i, 0], acts)
        gate = part if gate is None else gate + part
        part = dot(w_vmem[i, 1], acts)
        up = part if up is None else up + part
    gate, up = gate * inv, up * inv
    sigma = 1.0 / (1.0 + jnp.exp(-gate))
    grad_copy.wait()
    hid = grad_vmem[...].astype(f32)
    d_gate = hid * up * sigma * (1.0 + gate * (1.0 - sigma))
    d_up = hid * gate * sigma
    d_ref[0] = (d_gate * inv).astype(bf16)
    d_ref[1] = (d_up * inv).astype(bf16)
    hid_ref[0] = d_gate.astype(bf16)
    hid_ref[1] = d_up.astype(bf16)
    inner = jnp.sum(d_gate * gate + d_up * up, axis=0, keepdims=True)
    extra_ref[...] = jnp.concatenate(
        split_rows(inner)
        + split_rows(jnp.broadcast_to(amax, (1, tokens)))
        + [jnp.zeros((EXTRA - 6, tokens), f32)]
    ).astype(bf16)


def back_kernel(w_ref, hid_ref, extra_ref, mine_ref, other_ref, w_vmem, sems):
    arrivals = load_weights(w_ref, w_vmem, sems)
    tokens = hid_ref.shape[2]
    chans = mine_ref.shape[1]
    n_ctx, _, hidden, rows = w_ref.shape
    per = rows // chans
    cores = 2
    terms = n_ctx * per // cores * tokens
    mine_ref[terms:] = extra_ref[...]
    other_ref[terms:] = extra_ref[...]
    first = lax.axis_index("ch") % cores == 0
    rest = jnp.zeros((-hidden % 128, tokens), f32)
    d_gate, d_up = (
        jnp.concatenate([hid_ref[half].astype(f32), rest]).T.astype(bf16)[:, :hidden]
        for half in range(2)
    )
    step = 4
    for i in range(n_ctx):
        if i % step == 0:
            for arrival in arrivals[i : i + step]:
                arrival.wait()
        term = dot(d_gate, w_vmem[i, 0]) + dot(d_up, w_vmem[i, 1])
        for k in range(0, per, cores):
            even = term[:, k * chans : (k + 1) * chans]
            odd = term[:, (k + 1) * chans : (k + 2) * chans]
            start = (i * per + k) // cores * tokens
            mine_ref[start : start + tokens] = jnp.where(first, even, odd).astype(bf16)
            other_ref[start : start + tokens] = jnp.where(first, odd, even).astype(bf16)


def add_kernel(tokens, mine_ref, theirs_ref, piece_ref, sent_ref):
    chans = mine_ref.shape[1]
    pairs = sent_ref.shape[0]
    terms = pairs * tokens
    piece = piece_ref[...]
    inner, peak = None, None
    for met_ref in (mine_ref, theirs_ref):
        extra = met_ref[terms : terms + EXTRA].astype(f32)[:8]
        part = extra[0:1] + extra[1:2] + extra[2:3]
        top = extra[3:4] + extra[4:5] + extra[5:6]
        inner = part if inner is None else inner + part
        peak = top if peak is None else jnp.maximum(peak, top)
    extra = jnp.concatenate(
        split_rows(inner) + split_rows(peak) + [jnp.zeros((EXTRA - 6, chans), f32)]
    ).astype(bf16)
    for q in range(pairs):
        rows = slice(q * tokens, (q + 1) * tokens)
        total = mine_ref[rows].astype(f32) + theirs_ref[rows].astype(f32)
        sent_ref[q, :tokens] = total.astype(bf16)
        sent_ref[q, tokens : tokens + EXTRA] = extra
        sent_ref[q, tokens + EXTRA :] = piece


def norm_kernel(
    width, back_ref, r_ref, conv_ref, query_ref, gres_ref, gain_ref, inv_ref, dx_ref, dq_ref, sent_ref, mark_ref
):
    peers = back_ref.shape[0]
    chans, tokens = r_ref.shape
    n_ctx = sent_ref.shape[0]
    own = chans // n_ctx
    total = back_ref[0, :tokens].astype(f32)
    extra = back_ref[0, tokens : tokens + EXTRA].astype(f32)[:8]
    inner, peak = extra[0:1] + extra[1:2] + extra[2:3], extra[3:4] + extra[4:5] + extra[5:6]
    for peer in range(1, peers):
        total = total + back_ref[peer, :tokens].astype(f32)
        extra = back_ref[peer, tokens : tokens + EXTRA].astype(f32)[:8]
        inner = inner + (extra[0:1] + extra[1:2] + extra[2:3])
        peak = jnp.maximum(peak, extra[3:4] + extra[4:5] + extra[5:6])
    d_norm = total.T
    resid = r_ref[...]
    inv = inv_ref[...]
    gain = gain_ref[...]
    d_resid = (
        gres_ref[...].astype(f32).T
        + (gain * d_norm) * inv
        - resid * (inv * inv * inner / width)
    )
    dx_ref[...] = d_resid.T.astype(bf16)
    dq_ref[...] = (d_resid * conv_ref[...].astype(f32)).T.astype(bf16)
    d_conv = (d_resid * query_ref[...].astype(f32).T).astype(bf16).astype(f32)
    product = (d_norm * resid * inv).T
    gain_part = jnp.sum(product, axis=0, keepdims=True)
    mark_ref[...] = gain_part
    extra = split_rows(gain_part) + split_rows(peak) + [jnp.zeros((2, chans), f32)]
    for peer in range(n_ctx):
        rows = slice(peer * own, (peer + 1) * own)
        sent_ref[peer] = jnp.concatenate([d_conv[rows]] + extra).astype(bf16)


def rows_kernel(own_ref, other_ref, out_ref):
    peers, _, lanes = own_ref.shape
    blocks = out_ref.shape[0] // lanes
    own = lanes // blocks
    first = lax.axis_index("ch") % 2 == 0
    pieces = []
    for peer in range(peers):
        mine, theirs = own_ref[peer].astype(f32), other_ref[peer].astype(f32)
        pieces += [jnp.where(first, mine, theirs), jnp.where(first, theirs, mine)]
    for a in range(blocks):
        part = jnp.concatenate([piece[a * own : (a + 1) * own] for piece in pieces])
        out_ref[a * lanes : (a + 1) * lanes] = part.T.astype(bf16)


def grad_kernel(back_ref, fre_ref, fim_ref, *refs):
    tables = read_tables(refs[:7])
    ds_ref, gre_ref, gim_ref, dgain_ref, amax_ref = refs[7:]
    n_ctx = back_ref.shape[0]
    own = ds_ref.shape[0] // n_ctx
    blocks = [back_ref[k].astype(f32) for k in range(n_ctx)]
    real, imag = to_spectrum(jnp.concatenate([b[:own] for b in blocks]), tables, True)
    gre_ref[...], gim_ref[...] = real, imag
    fre, fim = fre_ref[...], fim_ref[...]
    back = from_spectrum(real * fre + imag * fim, imag * fre - real * fim, tables)
    ds_ref[...] = back.astype(bf16)
    gain, peak = None, None
    for block in blocks:
        extra = block[own:]
        g = extra[0:1] + extra[1:2] + extra[2:3]
        p = extra[3:4] + extra[4:5] + extra[5:6]
        gain = g if gain is None else gain + g
        peak = p if peak is None else jnp.maximum(peak, p)
    dgain_ref[...] = gain
    amax_ref[...] = jnp.max(peak, axis=1, keepdims=True)


def filter_grad_kernel(gre_ref, gim_ref, sre_ref, sim_ref, *refs):
    tables = read_tables(refs[:7])
    out_ref = refs[7]
    own = out_ref.shape[0]
    real, imag, sre, sim = gre_ref[...], gim_ref[...], sre_ref[...], sim_ref[...]
    grad = from_spectrum(real * sre + imag * sim, imag * sre - real * sim, tables)
    lanes = grad.shape[1]
    for a in range(out_ref.shape[1] // lanes):
        out_ref[:, a * lanes : (a + 1) * lanes] = grad[a * own : (a + 1) * own]


def products_kernel(ds_ref, key_ref, value_ref, dk_ref, dv_ref):
    grad = ds_ref[...].astype(f32).T
    dk_ref[...] = (grad * value_ref[...].astype(f32)).astype(bf16)
    dv_ref[...] = (grad * key_ref[...].astype(f32)).astype(bf16)


def weight_kernel(d_ref, rows_ref, first_ref, second_ref, d_vmem, out_vmem, sems, out_sems):
    n_ctx, _, _, tokens = d_ref.shape
    for copy in load_weights(d_ref, d_vmem, sems):
        copy.wait()
    stores = []
    for half, out_ref in enumerate((first_ref, second_ref)):
        part = jnp.concatenate([d_vmem[i, half] for i in range(n_ctx)], axis=1)
        out_vmem[half] = dot(part, rows_ref[...])
        store = pltpu.make_async_copy(out_vmem.at[half], out_ref, out_sems.at[half])
        store.start()
        stores.append(store)
    for store in stores:
        store.wait()


def on_device(resid_in, query_in, key_in, value_in, filt, gain, w_gate, w_up, g_hid, g_res):
    tokens, chans = resid_in.shape
    n_ctx = lax.axis_size("ctx")
    n_ch = lax.axis_size("ch")
    length = tokens * n_ctx
    rows, hidden = w_gate.shape
    own = chans // n_ctx
    tables = dft_tables(n_ctx, own, tokens)
    spec_rows = tables[6].shape[1]

    def in_hbm(array):
        return pltpu.with_memory_space_constraint(array, pltpu.HBM)

    tables = [in_hbm(jnp.asarray(table)) for table in tables]
    query_near = query_in
    key_in, value_in, resid_in, query_in, filt = (
        in_hbm(array) for array in (key_in, value_in, resid_in, query_in, filt)
    )
    spectrum = ((spec_rows, tokens), f32)
    square = ((chans, tokens), bf16)
    gain_col = gain[:, None]

    mixed, w_both = call(start_kernel, [square, ((2, hidden, rows), bf16)], 4, hbm=(0, 1))(
        key_in, value_in, in_hbm(w_gate.T), in_hbm(w_up.T)
    )
    w_all = in_hbm(lax.all_gather(w_both, "ctx", axis=0, tiled=False))
    spread = lax.all_to_all(mixed.reshape(n_ctx, own, tokens), "ctx", 0, 0, tiled=True)
    kept = [*tables, resid_in, query_in]
    fre, fim, fre_far, fim_far, *kept = call(
        filter_kernel,
        [spectrum] * 4 + [(array.shape, array.dtype) for array in kept],
        len(kept) + 1,
        vmem=(0, 1, *range(4, 4 + len(kept))),
        hbm=(2, 3),
    )(filt, *kept)
    conv, sre, sim = call(conv_kernel, [square, spectrum, spectrum], 10, hbm=(1, 2))(
        spread.reshape(chans, tokens), fre, fim, *kept[:7]
    )
    conv = lax.all_to_all(conv.reshape(n_ctx, own, tokens), "ctx", 0, 0, tiled=True).reshape(
        chans, tokens
    )
    sent, resid = call(
        resid_kernel,
        [((n_ch, chans + EXTRA, tokens), bf16), ((chans, tokens), f32)],
        4,
    )(conv, *kept[7:], gain_col)
    met = lax.all_to_all(sent, "ch", 0, 0, tiled=True)
    share = rows // n_ch
    per = chans // share
    my_ch = lax.axis_index("ch")
    piece = lax.dynamic_slice(
        met.reshape(n_ctx, n_ch // n_ctx, chans + EXTRA, tokens),
        (0, my_ch // per, my_ch % per * share, 0),
        (n_ctx, 1, share, tokens),
    ).reshape(n_ctx, share, tokens)
    piece = lax.all_to_all(piece, "ctx", 0, 0, tiled=True).reshape(n_ctx * share, tokens)
    met, piece = lax.optimization_barrier((met, piece))
    weights = (n_ctx, 2, hidden, rows)
    d_scaled, d_hid, inv, extra = call(
        hidden_kernel,
        [
            ((2, hidden, tokens), bf16),
            ((2, hidden, tokens), bf16),
            ((1, tokens), f32),
            ((EXTRA, tokens), bf16),
        ],
        5,
        in_specs=[VMEM, HBM, HBM, VMEM, VMEM],
        scratch=[
            pltpu.VMEM(weights, bf16),
            pltpu.VMEM((hidden, tokens), bf16),
            pltpu.SemaphoreType.DMA((n_ctx,)),
            pltpu.SemaphoreType.DMA(()),
        ],
        flops=1e9,
        limit=20,
        hbm=(0,),
    )(met, w_all, in_hbm(g_hid.T), resid, gain_col)
    d_all = in_hbm(lax.all_gather(d_scaled, "ctx", axis=0, tiled=False))
    cores = 2
    pairs = n_ch // cores
    piece_rows = n_ctx * share
    mine, theirs = call(
        back_kernel,
        [((pairs * tokens + EXTRA, chans), bf16)] * 2,
        3,
        in_specs=[HBM, VMEM, VMEM],
        scratch=[pltpu.VMEM(weights, bf16), pltpu.SemaphoreType.DMA((n_ctx,))],
        flops=1e9,
        limit=20,
    )(w_all, d_hid, extra)
    swap = [(j, j + 1 - 2 * (j % cores)) for j in range(n_ch)]
    plane = [[q * cores + core for q in range(pairs)] for core in range(cores)]
    theirs = lax.ppermute(theirs, "ch", swap)
    (sent,) = call(
        functools.partial(add_kernel, tokens),
        [((pairs, tokens + EXTRA + piece_rows, chans), bf16)],
        3,
        limit=16,
    )(mine, theirs, piece)
    back = lax.all_to_all(sent, "ch", 0, 0, tiled=True, axis_index_groups=plane)
    dx, dq, sent, mark = call(
        functools.partial(norm_kernel, chans * n_ch),
        [
            ((tokens, chans), bf16),
            ((tokens, chans), bf16),
            ((n_ctx, 2 * own, tokens), bf16),
            ((1, chans), f32),
        ],
        7,
    )(back, resid, conv, query_near, g_res, gain_col, inv)

    def reload(mark, arrays):
        return list(
            call(
                reload_kernel,
                [(array.shape, array.dtype) for array in arrays],
                len(arrays) + 1,
                vmem=range(len(arrays)),
            )(mark, *(in_hbm(array) for array in arrays))
        )

    mine, mark = lax.optimization_barrier((back[:, tokens + EXTRA :], mark))
    kept = reload(mark, [fre_far, fim_far, *tables])
    theirs = lax.ppermute(mine, "ch", swap)
    (row_acts,) = call(rows_kernel, [((length, rows), bf16)], 2)(mine, theirs)
    kept[0], row_acts = lax.optimization_barrier((kept[0], row_acts))
    back = lax.all_to_all(sent, "ctx", 0, 0, tiled=True)
    ds, gre, gim, dgain, amax = call(
        grad_kernel,
        [square, spectrum, spectrum, ((1, chans), f32), ((1, 1), f32)],
        10,
        hbm=(1, 2),
    )(back, *kept)
    ds = lax.all_to_all(ds.reshape(n_ctx, own, tokens), "ctx", 0, 0, tiled=True)
    (dfilt,) = call(filter_grad_kernel, [(filt.shape, f32)], 11)(
        *(in_hbm(array) for array in (gre, gim, sre, sim)), *tables
    )
    key_near, value_near = reload(dgain, [key_in, value_in])
    dk, dv = call(products_kernel, [((tokens, chans), bf16)] * 2, 3)(
        ds.reshape(chans, tokens), key_near, value_near
    )
    first, second = call(
        weight_kernel,
        [((hidden, rows), f32)] * 2,
        2,
        in_specs=[HBM, VMEM],
        out_specs=[HBM, HBM],
        scratch=[
            pltpu.VMEM((n_ctx, 2, hidden, tokens), bf16),
            pltpu.VMEM((2, hidden, rows), f32),
            pltpu.SemaphoreType.DMA((n_ctx,)),
            pltpu.SemaphoreType.DMA((2,)),
        ],
        hbm=(0, 1),
        flops=1e9,
        limit=16,
    )(d_all, row_acts)
    return (dx, dq, dk, dv, dfilt, dgain[0], first.T, second.T, amax[0, 0])


def solution(mesh):
    return jax.shard_map(
        on_device,
        mesh=mesh,
        in_specs=(
            P("ctx", "ch"),
            P("ctx", "ch"),
            P("ctx", "ch"),
            P("ctx", "ch"),
            P(("ch", "ctx"), None),
            P("ch"),
            P("ctx", "ch"),
            P("ctx", "ch"),
            P("ctx", "ch"),
            P("ctx", "ch"),
        ),
        out_specs=(
            P("ctx", "ch"),
            P("ctx", "ch"),
            P("ctx", "ch"),
            P("ctx", "ch"),
            P(("ch", "ctx"), None),
            P("ch"),
            P("ctx", "ch"),
            P("ctx", "ch"),
            P(),
        ),
        check_vma=False,
    )
```

```python
import functools
import math

import jax
import jax.numpy as jnp
import numpy as np
from jax import lax
from jax.experimental import pallas as pl
from jax.experimental.pallas import tpu as pltpu
from jax.sharding import PartitionSpec as P

epsilon = 1e-06
f32 = jnp.float32
bf16 = jnp.bfloat16
VMEM = pl.BlockSpec(memory_space=pltpu.VMEM)
HBM = pl.BlockSpec(memory_space=pltpu.HBM)
EXTRA = 16


def call(body, outs, n_in, flops=1e3, in_specs=None, out_specs=None, scratch=(), limit=8, hbm=(), vmem=()):
    return pl.pallas_call(
        body,
        out_shape=tuple(
            pltpu.HBM(s, d) if k in hbm else pltpu.VMEM(s, d) if k in vmem else jax.ShapeDtypeStruct(s, d)
            for k, (s, d) in enumerate(outs)
        ),
        in_specs=in_specs or [VMEM] * n_in,
        out_specs=tuple(out_specs or [VMEM] * len(outs)),
        scratch_shapes=list(scratch),
        compiler_params=pltpu.CompilerParams(vmem_limit_bytes=limit * 2**20),
        cost_estimate=pl.CostEstimate(flops=int(flops), bytes_accessed=int(flops / 1e3), transcendentals=0),
    )


def split_table(table):
    high = table.astype(np.float32).astype(jnp.bfloat16)
    low = (table - high.astype(np.float64)).astype(np.float32).astype(jnp.bfloat16)
    return np.asarray(high), np.asarray(low)


@functools.cache
def dft_tables(blocks, chans, lanes):
    turns = 2 * blocks
    half = blocks + 1
    total = turns * lanes
    freq = np.arange(half)
    eye = np.eye(chans)
    angle = 2.0 * np.pi * (np.outer(freq, np.arange(blocks)) % turns) / turns
    first = np.concatenate([np.kron(np.cos(angle), eye), np.kron(-np.sin(angle), eye)])
    weight = np.where((freq == 0) | (freq == blocks), 1.0, 2.0)[:, None] / total
    last = np.concatenate(
        [np.kron(weight * np.cos(angle), eye), np.kron(-weight * np.sin(angle), eye)]
    ).T
    angle = 2.0 * np.pi * (np.outer(np.arange(lanes), np.arange(lanes)) % lanes) / lanes
    inner = np.concatenate([np.cos(angle), np.sin(angle)], axis=1)
    angle = 2.0 * np.pi * np.repeat(np.outer(freq, np.arange(lanes)), chans, axis=0) / total
    twiddle = np.stack([np.cos(angle), np.sin(angle)]).astype(np.float32)
    last = np.pad(last, ((0, 0), (0, -last.shape[1] % lanes)))
    wide = [np.concatenate(np.split(t, t.shape[1] // lanes, axis=1)) for t in (last, inner)]
    return (*split_table(first), *split_table(wide[0]), *split_table(wide[1]), twiddle)


def read_tables(refs):
    tables = []
    for ref in refs:
        table = ref[...]
        if 2 <= len(tables) < 6:
            lanes = table.shape[1]
            table = jnp.concatenate(
                [table[k : k + lanes] for k in range(0, table.shape[0], lanes)], axis=1
            )
        tables.append(table)
    return tables


def pair(value):
    high = value.astype(bf16)
    return high, (value - high.astype(f32)).astype(bf16)


def dot(left, right):
    return jnp.dot(left, right, preferred_element_type=f32)


def turn_lanes(parts, inner_hi, inner_lo, lanes, sign):
    rows = parts.shape[0] // 2
    high, low = pair(parts)
    both = dot(high, inner_hi) + (dot(high, inner_lo) + dot(low, inner_hi))
    by_cos, by_sin = both[:, :lanes], both[:, lanes:]
    real = by_cos[:rows] - sign * by_sin[rows:]
    imag = by_cos[rows:] + sign * by_sin[:rows]
    return real, imag


def to_spectrum(signal, tables, exact):
    first_hi, first_lo, _, _, inner_hi, inner_lo, twiddle = tables
    lanes = signal.shape[1]
    if exact:
        signal = signal.astype(bf16)
        out = dot(first_hi, signal) + dot(first_lo, signal)
    else:
        high, low = pair(signal)
        out = dot(first_hi, high) + (dot(first_hi, low) + dot(first_lo, high))
    rows = out.shape[0] // 2
    real, imag = out[:rows], out[rows:]
    cos, sin = twiddle[0], twiddle[1]
    turned = jnp.concatenate([real * cos + imag * sin, imag * cos - real * sin])
    return turn_lanes(turned, inner_hi, inner_lo, lanes, -1.0)


def from_spectrum(real, imag, tables):
    _, _, last_hi, last_lo, inner_hi, inner_lo, twiddle = tables
    lanes = real.shape[1]
    real, imag = turn_lanes(jnp.concatenate([real, imag]), inner_hi, inner_lo, lanes, 1.0)
    cos, sin = twiddle[0], twiddle[1]
    both = jnp.concatenate([real * cos - imag * sin, real * sin + imag * cos])
    rest = jnp.zeros((last_hi.shape[1] - both.shape[0], lanes), f32)
    high, low = pair(jnp.concatenate([both, rest]))
    return dot(last_hi, high) + (dot(last_hi, low) + dot(last_lo, high))


def split_rows(row):
    high = row.astype(bf16).astype(f32)
    rest = row - high
    mid = rest.astype(bf16).astype(f32)
    low = rest - mid
    return [high, mid, low]


def start_kernel(key_ref, value_ref, gate_ref, up_ref, mixed_ref, w_ref):
    w_ref[0] = gate_ref[...]
    w_ref[1] = up_ref[...]
    mixed = (key_ref[...].astype(f32) * value_ref[...].astype(f32)).astype(bf16)
    mixed_ref[...] = mixed.astype(f32).T.astype(bf16)


def reload_kernel(mark_ref, *refs):
    half = len(refs) // 2
    for source, copy in zip(refs[:half], refs[half:]):
        copy[...] = source[...]


def filter_kernel(filt_ref, *refs):
    n_kept = (len(refs) - 4) // 2
    kept, spectra, copies = refs[:n_kept], refs[n_kept : n_kept + 4], refs[n_kept + 4 :]
    for source, copy in zip(kept, copies):
        copy[...] = source[...]
    tables = read_tables(kept[:7])
    lanes = kept[0].shape[1]
    blocks = filt_ref.shape[1] // lanes
    signal = jnp.concatenate([filt_ref[:, a * lanes : (a + 1) * lanes] for a in range(blocks)])
    real, imag = to_spectrum(signal, tables, False)
    for k in range(2):
        spectra[2 * k][...], spectra[2 * k + 1][...] = real, imag


def conv_kernel(src_ref, fre_ref, fim_ref, *refs):
    tables = read_tables(refs[:7])
    conv_ref, sre_ref, sim_ref = refs[7:]
    real, imag = to_spectrum(src_ref[...], tables, True)
    sre_ref[...], sim_ref[...] = real, imag
    fre, fim = fre_ref[...], fim_ref[...]
    conv = from_spectrum(real * fre - imag * fim, real * fim + imag * fre, tables)
    conv_ref[...] = conv.astype(bf16)


def resid_kernel(conv_ref, resid_ref, query_ref, gain_ref, sent_ref, r_ref):
    chans, tokens = conv_ref.shape
    resid = resid_ref[...].astype(f32).T + query_ref[...].astype(f32).T * conv_ref[...].astype(f32)
    r_ref[...] = resid
    scaled = (resid * gain_ref[...]).astype(bf16)
    square = jnp.sum(resid * resid, axis=0, keepdims=True)
    extra = jnp.concatenate(split_rows(square) + [jnp.zeros((EXTRA - 3, tokens), f32)]).astype(bf16)
    for peer in range(sent_ref.shape[0]):
        sent_ref[peer, :chans] = scaled
        sent_ref[peer, chans:] = extra


def load_weights(w_ref, w_vmem, sems):
    copies = [
        pltpu.make_async_copy(w_ref.at[i], w_vmem.at[i], sems.at[i]) for i in range(w_ref.shape[0])
    ]
    for copy in copies:
        copy.start()
    return copies


def hidden_kernel(
    met_ref, w_ref, grad_ref, r_ref, gain_ref, d_ref, hid_ref, inv_ref, extra_ref, w_vmem, grad_vmem, sems, grad_sem
):
    copies = load_weights(w_ref, w_vmem, sems)
    grad_copy = pltpu.make_async_copy(grad_ref, grad_vmem, grad_sem)
    grad_copy.start()
    n_ch, _, tokens = met_ref.shape
    chans = r_ref.shape[0]
    per = w_ref.shape[3] // chans
    total = jnp.zeros((8, tokens), f32)
    for peer in range(n_ch):
        total = total + met_ref[peer, chans : chans + EXTRA].astype(f32)[:8]
    inv = lax.rsqrt((total[0:1] + total[1:2] + total[2:3]) / (n_ch * chans) + epsilon)
    inv_ref[...] = inv
    amax = jnp.max(jnp.abs((r_ref[...] * gain_ref[...]) * inv), axis=0, keepdims=True)
    amax = jnp.max(amax, axis=1, keepdims=True)
    gate, up = None, None
    for i, copy in enumerate(copies):
        copy.wait()
        acts = jnp.concatenate([met_ref[i * per + k, :chans] for k in range(per)])
        part = dot(w_vmem[i, 0], acts)
        gate = part if gate is None else gate + part
        part = dot(w_vmem[i, 1], acts)
        up = part if up is None else up + part
    gate, up = gate * inv, up * inv
    sigma = 1.0 / (1.0 + jnp.exp(-gate))
    grad_copy.wait()
    hid = grad_vmem[...].astype(f32)
    d_gate = hid * up * sigma * (1.0 + gate * (1.0 - sigma))
    d_up = hid * gate * sigma
    d_ref[0] = (d_gate * inv).astype(bf16)
    d_ref[1] = (d_up * inv).astype(bf16)
    hid_ref[0] = d_gate.astype(bf16)
    hid_ref[1] = d_up.astype(bf16)
    inner = jnp.sum(d_gate * gate + d_up * up, axis=0, keepdims=True)
    extra_ref[...] = jnp.concatenate(
        split_rows(inner)
        + split_rows(jnp.broadcast_to(amax, (1, tokens)))
        + [jnp.zeros((EXTRA - 6, tokens), f32)]
    ).astype(bf16)


def back_kernel(w_ref, hid_ref, extra_ref, mine_ref, other_ref, w_vmem, sems):
    arrivals = load_weights(w_ref, w_vmem, sems)
    tokens = hid_ref.shape[2]
    chans = mine_ref.shape[1]
    n_ctx, _, hidden, rows = w_ref.shape
    per = rows // chans
    cores = 2
    terms = n_ctx * per // cores * tokens
    mine_ref[terms:] = extra_ref[...]
    other_ref[terms:] = extra_ref[...]
    first = lax.axis_index("ch") % cores == 0
    rest = jnp.zeros((-hidden % 128, tokens), f32)
    d_gate, d_up = (
        jnp.concatenate([hid_ref[half].astype(f32), rest]).T.astype(bf16)[:, :hidden]
        for half in range(2)
    )
    step = 4
    for i in range(n_ctx):
        if i % step == 0:
            for arrival in arrivals[i : i + step]:
                arrival.wait()
        term = dot(d_gate, w_vmem[i, 0]) + dot(d_up, w_vmem[i, 1])
        for k in range(0, per, cores):
            even = term[:, k * chans : (k + 1) * chans]
            odd = term[:, (k + 1) * chans : (k + 2) * chans]
            start = (i * per + k) // cores * tokens
            mine_ref[start : start + tokens] = jnp.where(first, even, odd).astype(bf16)
            other_ref[start : start + tokens] = jnp.where(first, odd, even).astype(bf16)


def add_kernel(tokens, mine_ref, theirs_ref, piece_ref, sent_ref):
    chans = mine_ref.shape[1]
    pairs = sent_ref.shape[0]
    terms = pairs * tokens
    piece = piece_ref[...]
    inner, peak = None, None
    for met_ref in (mine_ref, theirs_ref):
        extra = met_ref[terms : terms + EXTRA].astype(f32)[:8]
        part = extra[0:1] + extra[1:2] + extra[2:3]
        top = extra[3:4] + extra[4:5] + extra[5:6]
        inner = part if inner is None else inner + part
        peak = top if peak is None else jnp.maximum(peak, top)
    extra = jnp.concatenate(
        split_rows(inner) + split_rows(peak) + [jnp.zeros((EXTRA - 6, chans), f32)]
    ).astype(bf16)
    for q in range(pairs):
        rows = slice(q * tokens, (q + 1) * tokens)
        total = mine_ref[rows].astype(f32) + theirs_ref[rows].astype(f32)
        sent_ref[q, :tokens] = total.astype(bf16)
        sent_ref[q, tokens : tokens + EXTRA] = extra
        sent_ref[q, tokens + EXTRA :] = piece


def norm_kernel(
    width, back_ref, r_ref, conv_ref, query_ref, gres_ref, gain_ref, inv_ref, dx_ref, dq_ref, sent_ref, mark_ref
):
    peers = back_ref.shape[0]
    chans, tokens = r_ref.shape
    n_ctx = sent_ref.shape[0]
    own = chans // n_ctx
    total = back_ref[0, :tokens].astype(f32)
    extra = back_ref[0, tokens : tokens + EXTRA].astype(f32)[:8]
    inner, peak = extra[0:1] + extra[1:2] + extra[2:3], extra[3:4] + extra[4:5] + extra[5:6]
    for peer in range(1, peers):
        total = total + back_ref[peer, :tokens].astype(f32)
        extra = back_ref[peer, tokens : tokens + EXTRA].astype(f32)[:8]
        inner = inner + (extra[0:1] + extra[1:2] + extra[2:3])
        peak = jnp.maximum(peak, extra[3:4] + extra[4:5] + extra[5:6])
    d_norm = total.T
    resid = r_ref[...]
    inv = inv_ref[...]
    gain = gain_ref[...]
    d_resid = (
        gres_ref[...].astype(f32).T
        + (gain * d_norm) * inv
        - resid * (inv * inv * inner / width)
    )
    dx_ref[...] = d_resid.T.astype(bf16)
    dq_ref[...] = (d_resid * conv_ref[...].astype(f32)).T.astype(bf16)
    d_conv = (d_resid * query_ref[...].astype(f32).T).astype(bf16).astype(f32)
    product = (d_norm * resid * inv).T
    gain_part = jnp.sum(product, axis=0, keepdims=True)
    mark_ref[...] = gain_part
    extra = split_rows(gain_part) + split_rows(peak) + [jnp.zeros((2, chans), f32)]
    for peer in range(n_ctx):
        rows = slice(peer * own, (peer + 1) * own)
        sent_ref[peer] = jnp.concatenate([d_conv[rows]] + extra).astype(bf16)


def rows_kernel(own_ref, other_ref, out_ref):
    peers, _, lanes = own_ref.shape
    blocks = out_ref.shape[0] // lanes
    own = lanes // blocks
    first = lax.axis_index("ch") % 2 == 0
    pieces = []
    for peer in range(peers):
        mine, theirs = own_ref[peer].astype(f32), other_ref[peer].astype(f32)
        pieces += [jnp.where(first, mine, theirs), jnp.where(first, theirs, mine)]
    for a in range(blocks):
        part = jnp.concatenate([piece[a * own : (a + 1) * own] for piece in pieces])
        out_ref[a * lanes : (a + 1) * lanes] = part.T.astype(bf16)


def grad_kernel(back_ref, fre_ref, fim_ref, *refs):
    tables = read_tables(refs[:7])
    ds_ref, gre_ref, gim_ref, dgain_ref, amax_ref = refs[7:]
    n_ctx = back_ref.shape[0]
    own = ds_ref.shape[0] // n_ctx
    blocks = [back_ref[k].astype(f32) for k in range(n_ctx)]
    real, imag = to_spectrum(jnp.concatenate([b[:own] for b in blocks]), tables, True)
    gre_ref[...], gim_ref[...] = real, imag
    fre, fim = fre_ref[...], fim_ref[...]
    back = from_spectrum(real * fre + imag * fim, imag * fre - real * fim, tables)
    ds_ref[...] = back.astype(bf16)
    gain, peak = None, None
    for block in blocks:
        extra = block[own:]
        g = extra[0:1] + extra[1:2] + extra[2:3]
        p = extra[3:4] + extra[4:5] + extra[5:6]
        gain = g if gain is None else gain + g
        peak = p if peak is None else jnp.maximum(peak, p)
    dgain_ref[...] = gain
    amax_ref[...] = jnp.max(peak, axis=1, keepdims=True)


def filter_grad_kernel(gre_ref, gim_ref, sre_ref, sim_ref, *refs):
    tables = read_tables(refs[:7])
    out_ref = refs[7]
    own = out_ref.shape[0]
    real, imag, sre, sim = gre_ref[...], gim_ref[...], sre_ref[...], sim_ref[...]
    grad = from_spectrum(real * sre + imag * sim, imag * sre - real * sim, tables)
    lanes = grad.shape[1]
    for a in range(out_ref.shape[1] // lanes):
        out_ref[:, a * lanes : (a + 1) * lanes] = grad[a * own : (a + 1) * own]


def weight_kernel(
    d_ref, rows_ref, ds_ref, key_ref, value_ref, first_ref, second_ref, dk_ref, dv_ref, d_vmem, out_vmem, sems, out_sems
):
    n_ctx, _, _, tokens = d_ref.shape
    copies = load_weights(d_ref, d_vmem, sems)
    grad = ds_ref[...].astype(f32).T
    dk_ref[...] = (grad * value_ref[...].astype(f32)).astype(bf16)
    dv_ref[...] = (grad * key_ref[...].astype(f32)).astype(bf16)
    for copy in copies:
        copy.wait()
    stores = []
    for half, out_ref in enumerate((first_ref, second_ref)):
        part = jnp.concatenate([d_vmem[i, half] for i in range(n_ctx)], axis=1)
        out_vmem[half] = dot(part, rows_ref[...])
        store = pltpu.make_async_copy(out_vmem.at[half], out_ref, out_sems.at[half])
        store.start()
        stores.append(store)
    for store in stores:
        store.wait()


def on_device(resid_in, query_in, key_in, value_in, filt, gain, w_gate, w_up, g_hid, g_res):
    tokens, chans = resid_in.shape
    n_ctx = lax.axis_size("ctx")
    n_ch = lax.axis_size("ch")
    length = tokens * n_ctx
    rows, hidden = w_gate.shape
    own = chans // n_ctx
    tables = dft_tables(n_ctx, own, tokens)
    spec_rows = tables[6].shape[1]

    def in_hbm(array):
        return pltpu.with_memory_space_constraint(array, pltpu.HBM)

    tables = [in_hbm(jnp.asarray(table)) for table in tables]
    query_near = query_in
    key_in, value_in, resid_in, query_in, filt = (
        in_hbm(array) for array in (key_in, value_in, resid_in, query_in, filt)
    )
    spectrum = ((spec_rows, tokens), f32)
    square = ((chans, tokens), bf16)
    gain_col = gain[:, None]

    mixed, w_both = call(start_kernel, [square, ((2, hidden, rows), bf16)], 4, hbm=(0, 1))(
        key_in, value_in, in_hbm(w_gate.T), in_hbm(w_up.T)
    )
    w_all = in_hbm(lax.all_gather(w_both, "ctx", axis=0, tiled=False))
    spread = lax.all_to_all(mixed.reshape(n_ctx, own, tokens), "ctx", 0, 0, tiled=True)
    kept = [*tables, resid_in, query_in]
    fre, fim, fre_far, fim_far, *kept = call(
        filter_kernel,
        [spectrum] * 4 + [(array.shape, array.dtype) for array in kept],
        len(kept) + 1,
        vmem=(0, 1, *range(4, 4 + len(kept))),
        hbm=(2, 3),
    )(filt, *kept)
    conv, sre, sim = call(conv_kernel, [square, spectrum, spectrum], 10, hbm=(1, 2))(
        spread.reshape(chans, tokens), fre, fim, *kept[:7]
    )
    conv = lax.all_to_all(conv.reshape(n_ctx, own, tokens), "ctx", 0, 0, tiled=True).reshape(
        chans, tokens
    )
    sent, resid = call(
        resid_kernel,
        [((n_ch, chans + EXTRA, tokens), bf16), ((chans, tokens), f32)],
        4,
    )(conv, *kept[7:], gain_col)
    met = lax.all_to_all(sent, "ch", 0, 0, tiled=True)
    share = rows // n_ch
    per = chans // share
    my_ch = lax.axis_index("ch")
    piece = lax.dynamic_slice(
        met.reshape(n_ctx, n_ch // n_ctx, chans + EXTRA, tokens),
        (0, my_ch // per, my_ch % per * share, 0),
        (n_ctx, 1, share, tokens),
    ).reshape(n_ctx, share, tokens)
    piece = lax.all_to_all(piece, "ctx", 0, 0, tiled=True).reshape(n_ctx * share, tokens)
    met, piece = lax.optimization_barrier((met, piece))
    weights = (n_ctx, 2, hidden, rows)
    d_scaled, d_hid, inv, extra = call(
        hidden_kernel,
        [
            ((2, hidden, tokens), bf16),
            ((2, hidden, tokens), bf16),
            ((1, tokens), f32),
            ((EXTRA, tokens), bf16),
        ],
        5,
        in_specs=[VMEM, HBM, HBM, VMEM, VMEM],
        scratch=[
            pltpu.VMEM(weights, bf16),
            pltpu.VMEM((hidden, tokens), bf16),
            pltpu.SemaphoreType.DMA((n_ctx,)),
            pltpu.SemaphoreType.DMA(()),
        ],
        flops=1e9,
        limit=20,
        hbm=(0,),
    )(met, w_all, in_hbm(g_hid.T), resid, gain_col)
    d_all = in_hbm(lax.all_gather(d_scaled, "ctx", axis=0, tiled=False))
    cores = 2
    pairs = n_ch // cores
    piece_rows = n_ctx * share
    mine, theirs = call(
        back_kernel,
        [((pairs * tokens + EXTRA, chans), bf16)] * 2,
        3,
        in_specs=[HBM, VMEM, VMEM],
        scratch=[pltpu.VMEM(weights, bf16), pltpu.SemaphoreType.DMA((n_ctx,))],
        flops=1e9,
        limit=20,
    )(w_all, d_hid, extra)
    swap = [(j, j + 1 - 2 * (j % cores)) for j in range(n_ch)]
    plane = [[q * cores + core for q in range(pairs)] for core in range(cores)]
    theirs = lax.ppermute(theirs, "ch", swap)
    (sent,) = call(
        functools.partial(add_kernel, tokens),
        [((pairs, tokens + EXTRA + piece_rows, chans), bf16)],
        3,
        limit=16,
    )(mine, theirs, piece)
    back = lax.all_to_all(sent, "ch", 0, 0, tiled=True, axis_index_groups=plane)
    dx, dq, sent, mark = call(
        functools.partial(norm_kernel, chans * n_ch),
        [
            ((tokens, chans), bf16),
            ((tokens, chans), bf16),
            ((n_ctx, 2 * own, tokens), bf16),
            ((1, chans), f32),
        ],
        7,
    )(back, resid, conv, query_near, g_res, gain_col, inv)

    def reload(mark, arrays):
        return list(
            call(
                reload_kernel,
                [(array.shape, array.dtype) for array in arrays],
                len(arrays) + 1,
                vmem=range(len(arrays)),
            )(mark, *(in_hbm(array) for array in arrays))
        )

    mine, mark = lax.optimization_barrier((back[:, tokens + EXTRA :], mark))
    kept = reload(mark, [fre_far, fim_far, *tables])
    theirs = lax.ppermute(mine, "ch", swap)
    (row_acts,) = call(rows_kernel, [((length, rows), bf16)], 2)(mine, theirs)
    kept[0], row_acts = lax.optimization_barrier((kept[0], row_acts))
    back = lax.all_to_all(sent, "ctx", 0, 0, tiled=True)
    ds, gre, gim, dgain, amax = call(
        grad_kernel,
        [square, spectrum, spectrum, ((1, chans), f32), ((1, 1), f32)],
        10,
        hbm=(1, 2),
    )(back, *kept)
    ds = lax.all_to_all(ds.reshape(n_ctx, own, tokens), "ctx", 0, 0, tiled=True)
    (dfilt,) = call(filter_grad_kernel, [(filt.shape, f32)], 11)(
        *(in_hbm(array) for array in (gre, gim, sre, sim)), *tables
    )
    key_near, value_near = reload(dgain, [key_in, value_in])
    first, second, dk, dv = call(
        weight_kernel,
        [((hidden, rows), f32)] * 2 + [((tokens, chans), bf16)] * 2,
        5,
        in_specs=[HBM] + [VMEM] * 4,
        out_specs=[HBM, HBM, VMEM, VMEM],
        scratch=[
            pltpu.VMEM((n_ctx, 2, hidden, tokens), bf16),
            pltpu.VMEM((2, hidden, rows), f32),
            pltpu.SemaphoreType.DMA((n_ctx,)),
            pltpu.SemaphoreType.DMA((2,)),
        ],
        hbm=(0, 1),
        flops=1e9,
        limit=16,
    )(d_all, row_acts, ds.reshape(chans, tokens), key_near, value_near)
    return (dx, dq, dk, dv, dfilt, dgain[0], first.T, second.T, amax[0, 0])


def solution(mesh):
    return jax.shard_map(
        on_device,
        mesh=mesh,
        in_specs=(
            P("ctx", "ch"),
            P("ctx", "ch"),
            P("ctx", "ch"),
            P("ctx", "ch"),
            P(("ch", "ctx"), None),
            P("ch"),
            P("ctx", "ch"),
            P("ctx", "ch"),
            P("ctx", "ch"),
            P("ctx", "ch"),
        ),
        out_specs=(
            P("ctx", "ch"),
            P("ctx", "ch"),
            P("ctx", "ch"),
            P("ctx", "ch"),
            P(("ch", "ctx"), None),
            P("ch"),
            P("ctx", "ch"),
            P("ctx", "ch"),
            P(),
        ),
        check_vma=False,
    )
```
